256 devices in a mesh: img: 32 (over x, z), txt: 8 (over y, core).
Axes of the slice: x: 4, y: 4, z: 8, core: 2. Of those that a mesh axis runs over, the one named last changes fastest.
Arguments:
- images: bfloat16 [32768, 1024], P(('img', 'txt'))
- captions: bfloat16 [8192, 1024], P(('txt', 'img'))
- tile_mask: int32 [256, 64], P('img', 'txt'), may hold values from 0 to 1, as said below
Outputs:
- images_grad: float32 [32768, 1024], P(('img', 'txt'))
- captions_grad: float32 [8192, 1024], P(('txt', 'img'))
The draws below stay inside these ranges and needn't reach their ends.
Inputs may be any that keep to these rules, and one draw needn't show every extreme that they name: `tile_mask`: every row and every column of tiles holds at least one 1.
All inputs are finite; a program needn't handle non-finite values.
Results may differ from the reference program's by a relative error of at most 0.006.
Values may be sent and summed in bfloat16 or wider, within the bound.
No kernel may reach another device: no remote copies, remote signals or barrier semaphores. Data moves between devices by JAX's collectives and lax.ppermute only.
A program may use at most 64 MiB of HBM per device.

```python
import math
import jax
import jax.numpy as jnp
from jax import lax

D = 1024
BLK = 128
ITERS = 3
IMG_DEV = 1024
IMAGES = 32768
CAPTIONS = 8192
N_IMG = 32


def caption_table(key, jitter):
    base_key, noise_key = jax.random.split(key)
    base = jax.random.normal(base_key, (CAPTIONS // 2, D), jnp.float32) * 0.177
    noise = jax.random.normal(noise_key, (CAPTIONS // 2, D), jnp.float32)
    partner = jitter * noise
    return jnp.stack([base, partner], axis=1).reshape(CAPTIONS, D)


def draw_captions(key, part):
    table = caption_table(key, 0.177)
    return table.astype(jnp.bfloat16)


def draw_images(key, part):
    table = caption_table(key, 0.177)
    key = jax.random.fold_in(key, 11)
    first, second, third = jax.random.split(key, 3)
    index = jnp.arange(IMAGES)
    partner = index // BLK % (CAPTIONS // BLK) * BLK + index % BLK
    target = jax.random.uniform(third, (IMAGES, 1), jnp.float32, 5.0, 15.0)
    strength = target / (0.0313 * D)
    chosen = (index % 16 == 0)[:, None]
    scale = jnp.exp(jax.random.uniform(second, (IMAGES, 1), jnp.float32, -1.15, 1.15))
    own = jax.random.normal(first, (IMAGES, D), jnp.float32) * 0.177 * scale
    result = jnp.where(chosen, strength * table[partner], own)
    return result.astype(jnp.bfloat16)


def draw_tile_mask(key, part):
    key = jax.random.fold_in(key, 5)
    first, second = jax.random.split(key)
    tile_rows = IMAGES // BLK
    tile_cols = CAPTIONS // BLK
    rate = jax.random.randint(first, (tile_rows, 1), 1, 8)
    pick = jax.random.randint(second, (tile_rows, tile_cols), 0, 8)
    rows = jnp.arange(tile_rows)[:, None]
    cols = jnp.arange(tile_cols)[None, :]
    forced = cols == rows % tile_cols
    return jnp.where((pick < rate) | forced, 1, 0).astype(jnp.int32)


def setup_inputs(seed: int = 0) -> dict:
    arg_keys = jax.random.split(jax.random.key(seed), 4)
    images = draw_images(jax.random.fold_in(arg_keys[3], 71), 0)
    captions = draw_captions(jax.random.fold_in(arg_keys[3], 71), 0)
    tile_mask = draw_tile_mask(jax.random.fold_in(arg_keys[3], 71), 0)
    return {"images": images, "captions": captions, "tile_mask": tile_mask}


INVERSE_EPSILON = 4.0
NEG = -1e30


def expand(mask_rows):
    first, second = mask_rows.shape
    flags = jnp.broadcast_to(mask_rows[:, None, :, None] > 0, (first, BLK, second, BLK))
    return flags.reshape(first * BLK, second * BLK)


def plan_of(logits, keep, u_row, v_col, shift):
    return jnp.where(keep, jnp.exp(logits + u_row[:, None] + v_col[None, :] - shift), 0.0)


def reference(images, captions, tile_mask):
    log_ratio = math.log(IMAGES / CAPTIONS)
    img_blocks = images.reshape(N_IMG, IMG_DEV, D)
    mask_blocks = tile_mask.reshape(N_IMG, IMG_DEV // BLK, CAPTIONS // BLK)

    def scored(rows, mask_rows):
        similarity_scores = jnp.dot(rows, captions.T, preferred_element_type=jnp.float32)
        return similarity_scores, similarity_scores * INVERSE_EPSILON, expand(mask_rows)

    def sweep(v_col):
        def step(carry, block):
            top, total = carry
            similarity_scores, logits, keep = scored(block[0], block[1])
            z_row = jnp.where(keep, logits + v_col[None, :], NEG)
            m_row = jnp.max(z_row, axis=1)
            u_row = -(m_row + jnp.log(jnp.sum(jnp.exp(z_row - m_row[:, None]), axis=1)))
            w_col = jnp.where(keep, logits + u_row[:, None], NEG)
            newtop = jnp.maximum(top, jnp.max(w_col, axis=0))
            total = total * jnp.exp(top - newtop) + jnp.sum(jnp.exp(w_col - newtop[None, :]), axis=0)
            return (newtop, total), u_row

        init = (jnp.full((CAPTIONS,), NEG, jnp.float32), jnp.zeros((CAPTIONS,), jnp.float32))
        (top, total), u_all = lax.scan(step, init, (img_blocks, mask_blocks))
        return u_all.reshape(-1), log_ratio - (top + jnp.log(total))

    us = []
    vs = [jnp.zeros((CAPTIONS,), jnp.float32)]
    for step_index in range(ITERS):
        u_new, v_new = sweep(vs[-1])
        us.append(u_new)
        vs.append(v_new)
    u_blocks = [u.reshape(N_IMG, IMG_DEV) for u in us]
    last = ITERS - 1

    def first_pass(acc, block):
        similarity_scores, logits, keep = scored(block[0], block[1])
        transport_plan = plan_of(logits, keep, block[2], vs[ITERS], 0.0)
        return acc + jnp.sum(-similarity_scores * transport_plan, axis=0), None

    gv_last, unused = lax.scan(first_pass, jnp.zeros((CAPTIONS,), jnp.float32), (img_blocks, mask_blocks, u_blocks[last]))
    gvs = [None] * ITERS
    gus = [None] * ITERS
    gvs[last] = gv_last
    for k in range(last, 0, -1):
        def back_pass(acc, block, k=k):
            similarity_scores, logits, keep = scored(block[0], block[1])
            image_marginal_term = -gvs[k][None, :] * plan_of(logits, keep, block[2], vs[k + 1], log_ratio)
            if k == last:
                transport_plan = plan_of(logits, keep, block[2], vs[ITERS], 0.0)
                image_marginal_term = image_marginal_term - similarity_scores * transport_plan
            gu_row = jnp.sum(image_marginal_term, axis=1)
            caption_marginal_term = -gu_row[:, None] * plan_of(logits, keep, block[2], vs[k], 0.0)
            return acc + jnp.sum(caption_marginal_term, axis=0), gu_row

        gv_prev, gu_all = lax.scan(back_pass, jnp.zeros((CAPTIONS,), jnp.float32), (img_blocks, mask_blocks, u_blocks[k]))
        gus[k] = gu_all
        gvs[k - 1] = gv_prev

    def final_pass(acc, block):
        rows, mask_rows = block[0], block[1]
        similarity_scores, logits, keep = scored(rows, mask_rows)
        transport_plan = plan_of(logits, keep, block[2][last], vs[ITERS], 0.0)
        log_plan_gradient = -similarity_scores * transport_plan
        for k in range(ITERS):
            image_marginal_term = -gvs[k][None, :] * plan_of(logits, keep, block[2][k], vs[k + 1], log_ratio)
            if k == 0:
                gu_row = jnp.sum(image_marginal_term, axis=1)
            else:
                gu_row = block[3][k - 1]
            caption_marginal_term = -gu_row[:, None] * plan_of(logits, keep, block[2][k], vs[k], 0.0)
            log_plan_gradient = log_plan_gradient + image_marginal_term + caption_marginal_term
        similarity_gradient = (-transport_plan + INVERSE_EPSILON * log_plan_gradient).astype(jnp.bfloat16)
        img_grad = jnp.dot(similarity_gradient, captions, preferred_element_type=jnp.float32)
        acc = acc + jnp.dot(similarity_gradient.T, rows, preferred_element_type=jnp.float32)
        return acc, img_grad

    u_stack = jnp.stack(u_blocks, axis=1)
    gu_stack = jnp.stack(gus[1:], axis=1)
    captions_grad, img_grads = lax.scan(final_pass, jnp.zeros((CAPTIONS, D), jnp.float32), (img_blocks, mask_blocks, u_stack, gu_stack))
    return img_grads.reshape(IMAGES, D), captions_grad
```

```python
import functools

import jax
import jax.numpy as jnp
from jax import lax
from jax.experimental import pallas as pl
from jax.experimental.pallas import tpu as pltpu
from jax.sharding import Mesh, PartitionSpec as P

BLK = 128
INVERSE_EPSILON = 4.0
NEG = -1e30
X, Z, Y, C = 4, 8, 4, 2
N_IMG, N_TXT = X * Z, Y * C
TILES = 8
SIDE = TILES * BLK
F32, BF16 = jnp.float32, jnp.bfloat16
RATIO = 4.0

VMEM = pl.BlockSpec(memory_space=pltpu.VMEM)
SMEM = pl.BlockSpec(memory_space=pltpu.SMEM)
MIB = 1024 * 1024


def tile(index):
    return pl.ds(index * BLK, BLK)


def spread_rows(vec_ref, out_ref):
    for q in range(TILES):
        row = jnp.broadcast_to(vec_ref[q : q + 1, :], (BLK, BLK))
        out_ref[tile(q), :] = row.T


def put_all(out_ref, slot, q, row):
    for peer in range(out_ref.shape[0]):
        out_ref[peer, slot, q : q + 1, :] = row


def row_totals(out_ref, slot, term):
    for q in range(TILES):
        total = term(q, 0)
        for t in range(1, TILES):
            total = total + term(q, t)
        put_all(out_ref, slot, q, jnp.sum(total.T, axis=0, keepdims=True))


def col_totals(out_ref, slot, term, scale):
    for t in range(TILES):
        total = term(0, t)
        for q in range(1, TILES):
            total = total + term(q, t)
        put_all(out_ref, slot, t, jnp.sum(total, axis=0, keepdims=True) * scale[t : t + 1, :])


def scores_kernel(pos, mask, i0, i1, i2, i3, j0, j1, j2, j3, c0, c1, c2, c3, img, cap, s, stats):
    x, y, core = pos[0], pos[2], pos[3]
    for k, (own, other) in enumerate(((i0, j0), (i1, j1), (i2, j2), (i3, j3))):
        source = lax.rem(y - k + Y, Y)
        img[pl.ds((source * 2 + core) * BLK, BLK), :] = own[...]
        img[pl.ds((source * 2 + 1 - core) * BLK, BLK), :] = other[...]
    for k, piece in enumerate((c0, c1, c2, c3)):
        source = lax.rem(x - k + X, X)
        cap[pl.ds(source * 256, 256), :] = piece[...]
    for q2 in range(TILES // 2):
        rows = pl.ds(q2 * 256, 256)
        s[rows, :] = lax.dot_general(
            img[rows, :], cap[...], (((1,), (1,)), ((), ())), preferred_element_type=F32
        )
        for q in (2 * q2, 2 * q2 + 1):
            top = jnp.full((BLK, BLK), NEG, F32)
            for t in range(TILES):
                z = jnp.where(mask[q, t] > 0, s[tile(q), tile(t)] * INVERSE_EPSILON, NEG)
                top = jnp.maximum(top, z)
            top_col = jnp.max(top, axis=1, keepdims=True)
            total = jnp.zeros((BLK, BLK), F32)
            for t in range(TILES):
                z = jnp.where(mask[q, t] > 0, s[tile(q), tile(t)] * INVERSE_EPSILON, NEG)
                total = total + jnp.exp(z - top_col)
            put_all(stats, 0, q, jnp.max(top.T, axis=0, keepdims=True))
            put_all(stats, 1, q, jnp.sum(total.T, axis=0, keepdims=True))


def joined(stats):
    top = jnp.max(stats[:, 0], axis=0)
    total = jnp.sum(stats[:, 1] * jnp.exp(stats[:, 0] - top[None]), axis=0)
    return top, total


def kernel_matrix(mask, row_stats, s, e, stats, top_out, u_vec, u_rows):
    top, total = joined(row_stats)
    u_vec[...] = -(top + jnp.log(total))
    spread_rows(u_vec, u_rows)
    for t in range(TILES):
        top = jnp.full((BLK, BLK), NEG, F32)
        for q in range(TILES):
            w = s[tile(q), tile(t)] * INVERSE_EPSILON + u_rows[tile(q), :]
            top = jnp.maximum(top, jnp.where(mask[q, t] > 0, w, NEG))
        top_row = jnp.max(top, axis=0, keepdims=True)
        total = jnp.zeros((BLK, BLK), F32)
        for q in range(TILES):
            w = s[tile(q), tile(t)] * INVERSE_EPSILON + u_rows[tile(q), :]
            value = jnp.where(mask[q, t] > 0, jnp.exp(jnp.where(mask[q, t] > 0, w, NEG) - top_row), 0.0)
            e[tile(q), tile(t)] = value
            total = total + value
        top_out[t : t + 1, :] = top_row
        put_all(stats, 0, t, top_row)
        put_all(stats, 1, t, jnp.sum(total, axis=0, keepdims=True))


def first_row_pass(col_stats, own_top, e, x, f, fb0):
    top, total = joined(col_stats)
    mine = own_top[...]
    f[...] = RATIO * jnp.exp(mine - top) / total
    fb0[...] = jnp.exp(mine)
    row_totals(x, 0, lambda q, t: e[tile(q), tile(t)] * f[t : t + 1, :])


def col_pass(x_all, f, e, y, a, rows):
    a[...] = 1.0 / jnp.sum(x_all[:, 0], axis=0)
    spread_rows(a, rows)
    col_totals(y, 0, lambda q, t: e[tile(q), tile(t)] * rows[tile(q), :], f[...])


def row_pass(y_all, f, e, x, b, fb):
    b[...] = RATIO / jnp.sum(y_all[:, 0], axis=0)
    fb[...] = f[...] * b[...]
    row_totals(x, 0, lambda q, t: e[tile(q), tile(t)] * fb[t : t + 1, :])


def last_col_pass(x_all, f, e, s, y, a, rows):
    a[...] = 1.0 / jnp.sum(x_all[:, 0], axis=0)
    spread_rows(a, rows)
    scale = f[...]
    for t in range(TILES):
        total = jnp.zeros((BLK, BLK), F32)
        scored = jnp.zeros((BLK, BLK), F32)
        for q in range(TILES):
            value = e[tile(q), tile(t)] * rows[tile(q), :]
            total = total + value
            scored = scored + value * s[tile(q), tile(t)]
        put_all(y, 0, t, jnp.sum(total, axis=0, keepdims=True) * scale[t : t + 1, :])
        put_all(y, 1, t, jnp.sum(scored, axis=0, keepdims=True) * scale[t : t + 1, :])


def gu3_pass(y_all, f, a3, e, s, x, b3, gv3, c0, c1):
    b3[...] = RATIO / jnp.sum(y_all[:, 0], axis=0)
    gv3[...] = -b3[...] * jnp.sum(y_all[:, 1], axis=0)
    c1[...] = f[...] * b3[...]
    c0[...] = c1[...] * gv3[...] * (1.0 / RATIO)
    row_totals(
        x, 0, lambda q, t: e[tile(q), tile(t)] * (s[tile(q), tile(t)] * c1[t : t + 1, :] + c0[t : t + 1, :])
    )


def gv_pass(x_all, a, f, b, e, y, agu, rows, *, scale):
    gu = -scale * a[...] * jnp.sum(x_all[:, 0], axis=0)
    agu[...] = a[...] * gu
    spread_rows(agu, rows)
    col_totals(y, 0, lambda q, t: e[tile(q), tile(t)] * rows[tile(q), :], -(f[...] * b[...]))


def gu_pass(y_all, f, b, e, x, bgv, c):
    bgv[...] = b[...] * jnp.sum(y_all[:, 0], axis=0)
    c[...] = f[...] * bgv[...]
    row_totals(x, 0, lambda q, t: e[tile(q), tile(t)] * c[t : t + 1, :])


def captions_kernel(
    pos, x_all, a2, a3, agu2, agu3, f, fb0, b2, b3, gv3, bgv2, gv1, e, s, img,
    gs, o0, o1, o2, o3, vec, r_a3, r_a2, r_gu3, r_gu2, r_gu1,
):
    spread_rows(a3, r_a3)
    spread_rows(a2, r_a2)
    vec[...] = INVERSE_EPSILON * agu3[...]
    spread_rows(vec, r_gu3)
    vec[...] = INVERSE_EPSILON * agu2[...]
    spread_rows(vec, r_gu2)
    vec[...] = (-INVERSE_EPSILON / RATIO) * jnp.sum(x_all[:, 0], axis=0)
    spread_rows(vec, r_gu1)
    scale = f[...]
    k_s = -INVERSE_EPSILON * (scale * b3[...])
    k_a3 = -(scale * b3[...]) * (1.0 + gv3[...])
    k_a2 = -scale * bgv2[...]
    k_1 = -scale * gv1[...]
    k_gu3 = -scale * b2[...]
    k_gu2 = -scale
    k_gu1 = -fb0[...]
    for t in range(TILES):
        pick = slice(t, t + 1)
        for q in range(TILES):
            rows = tile(q)
            value = (
                r_a3[rows, :] * (k_a3[pick, :] + k_s[pick, :] * s[rows, tile(t)])
                + r_a2[rows, :] * k_a2[pick, :]
                + k_1[pick, :]
                + r_gu3[rows, :] * k_gu3[pick, :]
                + r_gu2[rows, :] * k_gu2[pick, :]
                + r_gu1[rows, :] * k_gu1[pick, :]
            )
            gs[rows, tile(t)] = (value * e[rows, tile(t)]).astype(BF16)
    x = pos[0]
    for k, out in enumerate((o0, o1, o2, o3)):
        target = lax.rem(x + k, X)
        columns = pl.ds(pl.multiple_of(target * 256, 256), 256)
        out[...] = lax.dot_general(
            gs[:, columns], img[...], (((0,), (0,)), ((), ())), preferred_element_type=F32
        ).astype(BF16)


def images_kernel(pos, gs, cap, mine, other):
    core = pos[3]
    for y in range(Y):
        for out, c in ((mine, core), (other, 1 - core)):
            out[y] = jnp.dot(
                gs[pl.ds((y * 2 + c) * BLK, BLK), :], cap[...], preferred_element_type=F32
            ).astype(out.dtype)


def shape(dims, dtype=F32):
    return jax.ShapeDtypeStruct(dims, dtype)


VEC = (TILES, BLK)
ROWS = pltpu.VMEM((SIDE, BLK), F32)


def run(kernel, outs, scratch, smem, *args, limit=24):
    return pl.pallas_call(
        kernel,
        out_shape=outs,
        in_specs=[SMEM] * smem + [VMEM] * (len(args) - smem),
        out_specs=[VMEM] * len(outs),
        scratch_shapes=scratch,
        compiler_params=pltpu.CompilerParams(vmem_limit_bytes=limit * MIB),
    )(*args)


def ring(n, k):
    return [(i, (i + k) % n) for i in range(n)]


def over_txt(v):
    return lax.all_to_all(v, ("y", "c"), 0, 0, tiled=True)


def over_img(v):
    return lax.all_to_all(v, ("x", "z"), 0, 0, tiled=True)


def on_device(images, captions, tile_mask):
    pos = jnp.stack([lax.axis_index(name) for name in ("x", "z", "y", "c")]).astype(jnp.int32)
    own = [images] + [lax.ppermute(images, "y", ring(Y, k)) for k in range(1, Y)]
    other = [lax.ppermute(piece, "c", ring(C, 1)) for piece in own]
    cap_z = lax.all_to_all(
        jnp.broadcast_to(captions[None], (Z,) + captions.shape), "z", 0, 0, tiled=True
    ).reshape(256, SIDE)
    caps = [cap_z] + [lax.ppermute(cap_z, "x", ring(X, k)) for k in range(1, X)]

    to_txt = shape((N_TXT, 1) + VEC)
    to_img = shape((N_IMG, 1) + VEC)
    square = (SIDE, SIDE)
    img, cap, s, row_stats = run(
        scores_kernel,
        [shape(square, BF16), shape(square, BF16), shape(square), shape((N_TXT, 2) + VEC)],
        [], 2, pos, tile_mask, *own, *other, *caps, limit=32,
    )
    e, col_stats, top = run(
        kernel_matrix, [shape(square), shape((N_IMG, 2) + VEC), shape(VEC)],
        [pltpu.VMEM(VEC, F32), ROWS], 1, tile_mask, over_txt(row_stats), s,
    )
    x, f, fb0 = run(first_row_pass, [to_txt, shape(VEC), shape(VEC)], [], 0, over_img(col_stats), top, e)
    y, a2 = run(col_pass, [to_img, shape(VEC)], [ROWS], 0, over_txt(x), f, e)
    vec = pltpu.VMEM(VEC, F32)
    x, b2 = run(row_pass, [to_txt, shape(VEC)], [vec], 0, over_img(y), f, e)
    y, a3 = run(last_col_pass, [shape((N_IMG, 2) + VEC), shape(VEC)], [ROWS], 0, over_txt(x), f, e, s)
    x, b3, gv3 = run(gu3_pass, [to_txt, shape(VEC), shape(VEC)], [vec, vec], 0, over_img(y), f, a3, e, s)
    y, agu3 = run(functools.partial(gv_pass, scale=1.0), [to_img, shape(VEC)], [ROWS], 0, over_txt(x), a3, f, b2, e)
    x, bgv2 = run(gu_pass, [to_txt, shape(VEC)], [vec], 0, over_img(y), f, b2, e)
    one = jnp.ones(VEC, F32)
    y, agu2 = run(functools.partial(gv_pass, scale=1.0 / RATIO), [to_img, shape(VEC)], [ROWS], 0, over_txt(x), a2, f, one, e)
    x, gv1 = run(gu_pass, [to_txt, shape(VEC)], [vec], 0, over_img(y), f, one, e)
    gs, o0, o1, o2, o3 = run(
        captions_kernel, [shape(square, BF16)] + [shape((256, SIDE), BF16)] * X,
        [vec] + [ROWS] * 5, 1,
        pos, over_txt(x), a2, a3, agu2, agu3, f, fb0, b2, b3, gv3, bgv2, gv1, e, s, img, limit=32,
    )
    total = o0.astype(F32)
    for k, out in enumerate((o1, o2, o3), 1):
        total = total + lax.ppermute(out, "x", ring(X, k)).astype(F32)
    half = (Y, BLK, SIDE)
    mine, sibling = run(images_kernel, [shape(half, F32), shape(half, BF16)], [], 1, pos, gs, cap, limit=32)
    half_sum = mine + lax.ppermute(sibling, "c", ring(C, 1)).astype(F32)
    y_index = lax.axis_index("y")
    images_grad = lax.dynamic_index_in_dim(half_sum, y_index, 0, keepdims=False)
    sent = half_sum.astype(BF16)
    for k in range(1, Y):
        piece = lax.dynamic_index_in_dim(sent, lax.rem(y_index + k, Y), 0, keepdims=False)
        images_grad = images_grad + lax.ppermute(piece, "y", ring(Y, k)).astype(F32)
    parts = lax.all_to_all(total.astype(BF16).reshape(Z, 32, SIDE), "z", 0, 0, tiled=True)
    captions_grad = jnp.sum(parts.astype(F32), axis=0)
    return (images_grad, captions_grad)


def solution(mesh):
    split = Mesh(mesh.devices.reshape(X, Z, Y, C), ("x", "z", "y", "c"))
    img, txt = ("x", "z"), ("y", "c")
    in_specs = (P(img + txt, None), P(txt + img, None), P(img, txt))
    out_specs = (P(img + txt, None), P(txt + img, None))
    return jax.shard_map(on_device, mesh=split, in_specs=in_specs, out_specs=out_specs, check_vma=False)
```

```python
import functools

import jax
import jax.numpy as jnp
from jax import lax
from jax.experimental import pallas as pl
from jax.experimental.pallas import tpu as pltpu
from jax.sharding import Mesh, PartitionSpec as P

BLK = 128
INVERSE_EPSILON = 4.0
NEG = -1e30
X, ZH, ZL, Y, C = 4, 4, 2, 4, 2
N_IMG, N_TXT = X * ZH * C, Y * ZL
TILES = 8
SIDE = TILES * BLK
F32, BF16 = jnp.float32, jnp.bfloat16
RATIO = 4.0

VMEM = pl.BlockSpec(memory_space=pltpu.VMEM)
SMEM = pl.BlockSpec(memory_space=pltpu.SMEM)
MIB = 1024 * 1024


def tile(index):
    return pl.ds(index * BLK, BLK)


def spread_rows(vec_ref, out_ref):
    for q in range(TILES):
        row = jnp.broadcast_to(vec_ref[q : q + 1, :], (BLK, BLK))
        out_ref[tile(q), :] = row.T


def put_all(out_ref, slot, q, row):
    for peer in range(out_ref.shape[0]):
        out_ref[peer, slot, q : q + 1, :] = row


def row_totals(out_ref, slot, term):
    for q in range(TILES):
        total = term(q, 0)
        for t in range(1, TILES):
            total = total + term(q, t)
        put_all(out_ref, slot, q, jnp.sum(total.T, axis=0, keepdims=True))


def col_totals(out_ref, slot, term, scale):
    for t in range(TILES):
        total = term(0, t)
        for q in range(1, TILES):
            total = total + term(q, t)
        put_all(out_ref, slot, t, jnp.sum(total, axis=0, keepdims=True) * scale[t : t + 1, :])


def kept(mask, q, t):
    return jnp.broadcast_to(mask[q * TILES + t : q * TILES + t + 1, :], (BLK, BLK)) > 0


def spread_mask(pos, m00, m01, m10, m11, mask):
    zl, c = pos[2], pos[4]
    left = lax.broadcasted_iota(jnp.int32, (1, BLK), 1) < BLK // 2
    for y in range(Y):
        for dz in range(ZL):
            row = y * 2 + c
            q = y * 2 + jnp.where(dz == 0, zl, 1 - zl)
            for dc, flags in enumerate((m10, m11) if dz else (m00, m01)):
                column = jnp.where(dc == 0, c, 1 - c)
                for x in range(X):
                    lanes = jnp.where(left, flags[row, 2 * x], flags[row, 2 * x + 1])
                    mask[pl.ds(q * TILES + column * X + x, 1), :] = lanes.astype(F32)


def scores_kernel(
    pos, m00, m01, m10, m11, i0, i1, i2, i3, c0, c1, c2, c3, d0, d1, d2, d3, img, cap, s, stats, mask
):
    x, zh, zl, y, c = pos[0], pos[1], pos[2], pos[3], pos[4]
    spread_mask(pos, m00, m01, m10, m11, mask)
    for k, pieces in enumerate((i0, i1, i2, i3)):
        source = lax.rem(y - k + Y, Y)
        for slot in range(2):
            half = jnp.where(slot == 0, zl, 1 - zl)
            img[pl.ds((source * 2 + half) * BLK, BLK), :] = pieces[slot]
    for k, (own, other) in enumerate(((c0, d0), (c1, d1), (c2, d2), (c3, d3))):
        source = lax.rem(x - k + X, X)
        for j in range(ZH):
            place = lax.rem(zh - j + ZH, ZH) * 32
            cap[pl.ds((c * X + source) * BLK + place, 32), :] = own[j]
            cap[pl.ds(((1 - c) * X + source) * BLK + place, 32), :] = other[j]
    for q2 in range(TILES // 2):
        rows = pl.ds(q2 * 256, 256)
        s[rows, :] = lax.dot_general(
            img[rows, :], cap[...], (((1,), (1,)), ((), ())), preferred_element_type=F32
        )
        for q in (2 * q2, 2 * q2 + 1):
            top = jnp.full((BLK, BLK), NEG, F32)
            for t in range(TILES):
                z = jnp.where(kept(mask, q, t), s[tile(q), tile(t)] * INVERSE_EPSILON, NEG)
                top = jnp.maximum(top, z)
            top_col = jnp.max(top, axis=1, keepdims=True)
            total = jnp.zeros((BLK, BLK), F32)
            for t in range(TILES):
                z = jnp.where(kept(mask, q, t), s[tile(q), tile(t)] * INVERSE_EPSILON, NEG)
                total = total + jnp.exp(z - top_col)
            put_all(stats, 0, q, jnp.max(top.T, axis=0, keepdims=True))
            put_all(stats, 1, q, jnp.sum(total.T, axis=0, keepdims=True))


def joined(stats):
    top = jnp.max(stats[:, 0], axis=0)
    total = jnp.sum(stats[:, 1] * jnp.exp(stats[:, 0] - top[None]), axis=0)
    return top, total


def kernel_matrix(mask, row_stats, s, e, stats, top_out, u_vec, u_rows):
    top, total = joined(row_stats)
    u_vec[...] = -(top + jnp.log(total))
    spread_rows(u_vec, u_rows)
    for t in range(TILES):
        top = jnp.full((BLK, BLK), NEG, F32)
        for q in range(TILES):
            w = s[tile(q), tile(t)] * INVERSE_EPSILON + u_rows[tile(q), :]
            top = jnp.maximum(top, jnp.where(kept(mask, q, t), w, NEG))
        top_row = jnp.max(top, axis=0, keepdims=True)
        total = jnp.zeros((BLK, BLK), F32)
        for q in range(TILES):
            w = s[tile(q), tile(t)] * INVERSE_EPSILON + u_rows[tile(q), :]
            keep = kept(mask, q, t)
            value = jnp.where(keep, jnp.exp(jnp.where(keep, w, NEG) - top_row), 0.0)
            e[tile(q), tile(t)] = value
            total = total + value
        top_out[t : t + 1, :] = top_row
        put_all(stats, 0, t, top_row)
        put_all(stats, 1, t, jnp.sum(total, axis=0, keepdims=True))


def first_row_pass(col_stats, own_top, e, x, f, fb0):
    top, total = joined(col_stats)
    mine = own_top[...]
    f[...] = RATIO * jnp.exp(mine - top) / total
    fb0[...] = jnp.exp(mine)
    row_totals(x, 0, lambda q, t: e[tile(q), tile(t)] * f[t : t + 1, :])


def col_pass(x_all, f, e, y, a, rows):
    a[...] = 1.0 / jnp.sum(x_all[:, 0], axis=0)
    spread_rows(a, rows)
    col_totals(y, 0, lambda q, t: e[tile(q), tile(t)] * rows[tile(q), :], f[...])


def row_pass(y_all, f, e, x, b, fb):
    b[...] = RATIO / jnp.sum(y_all[:, 0], axis=0)
    fb[...] = f[...] * b[...]
    row_totals(x, 0, lambda q, t: e[tile(q), tile(t)] * fb[t : t + 1, :])


def last_col_pass(x_all, f, e, s, y, a, rows):
    a[...] = 1.0 / jnp.sum(x_all[:, 0], axis=0)
    spread_rows(a, rows)
    scale = f[...]
    for t in range(TILES):
        total = jnp.zeros((BLK, BLK), F32)
        scored = jnp.zeros((BLK, BLK), F32)
        for q in range(TILES):
            value = e[tile(q), tile(t)] * rows[tile(q), :]
            total = total + value
            scored = scored + value * s[tile(q), tile(t)]
        put_all(y, 0, t, jnp.sum(total, axis=0, keepdims=True) * scale[t : t + 1, :])
        put_all(y, 1, t, jnp.sum(scored, axis=0, keepdims=True) * scale[t : t + 1, :])


def gu3_pass(y_all, f, a3, e, s, x, b3, gv3, c0, c1):
    b3[...] = RATIO / jnp.sum(y_all[:, 0], axis=0)
    gv3[...] = -b3[...] * jnp.sum(y_all[:, 1], axis=0)
    c1[...] = f[...] * b3[...]
    c0[...] = c1[...] * gv3[...] * (1.0 / RATIO)
    row_totals(
        x, 0, lambda q, t: e[tile(q), tile(t)] * (s[tile(q), tile(t)] * c1[t : t + 1, :] + c0[t : t + 1, :])
    )


def gv_pass(x_all, a, f, b, e, y, agu, rows, *, scale):
    gu = -scale * a[...] * jnp.sum(x_all[:, 0], axis=0)
    agu[...] = a[...] * gu
    spread_rows(agu, rows)
    col_totals(y, 0, lambda q, t: e[tile(q), tile(t)] * rows[tile(q), :], -(f[...] * b[...]))


def gu_pass(y_all, f, b, e, x, bgv, c):
    bgv[...] = b[...] * jnp.sum(y_all[:, 0], axis=0)
    c[...] = f[...] * bgv[...]
    row_totals(x, 0, lambda q, t: e[tile(q), tile(t)] * c[t : t + 1, :])


def captions_kernel(
    pos, x_all, a2, a3, agu2, agu3, f, fb0, b2, b3, gv3, bgv2, gv1, e, s, img,
    gs, mine, other, vec, r_a3, r_a2, r_gu3, r_gu2, r_gu1,
):
    spread_rows(a3, r_a3)
    spread_rows(a2, r_a2)
    vec[...] = INVERSE_EPSILON * agu3[...]
    spread_rows(vec, r_gu3)
    vec[...] = INVERSE_EPSILON * agu2[...]
    spread_rows(vec, r_gu2)
    vec[...] = (-INVERSE_EPSILON / RATIO) * jnp.sum(x_all[:, 0], axis=0)
    spread_rows(vec, r_gu1)
    scale = f[...]
    k_s = -INVERSE_EPSILON * (scale * b3[...])
    k_a3 = -(scale * b3[...]) * (1.0 + gv3[...])
    k_a2 = -scale * bgv2[...]
    k_1 = -scale * gv1[...]
    k_gu3 = -scale * b2[...]
    k_gu2 = -scale
    k_gu1 = -fb0[...]
    for t in range(TILES):
        pick = slice(t, t + 1)
        for q in range(TILES):
            rows = tile(q)
            value = (
                r_a3[rows, :] * (k_a3[pick, :] + k_s[pick, :] * s[rows, tile(t)])
                + r_a2[rows, :] * k_a2[pick, :]
                + k_1[pick, :]
                + r_gu3[rows, :] * k_gu3[pick, :]
                + r_gu2[rows, :] * k_gu2[pick, :]
                + r_gu1[rows, :] * k_gu1[pick, :]
            )
            gs[rows, tile(t)] = (value * e[rows, tile(t)]).astype(BF16)
    core = pos[4]
    for out, c in ((other, 1 - core), (mine, core)):
        for half in range(2):
            columns = pl.ds(pl.multiple_of(c * 512 + half * 256, 256), 256)
            out[half * 256 : half * 256 + 256, :] = lax.dot_general(
                gs[:, columns], img[...], (((0,), (0,)), ((), ())), preferred_element_type=F32
            ).astype(out.dtype)


def images_kernel(pos, gs, cap, o0, o1, o3, o2a, o2b):
    y = pos[3]
    for k, out in ((2, None), (1, o1), (3, o3), (0, o0)):
        target = lax.rem(y + k, Y)
        value = jnp.dot(gs[pl.ds(target * 256, 256), :], cap[...], preferred_element_type=F32)
        if k == 2:
            o2a[...] = value[:BLK].astype(BF16)
            o2b[...] = value[BLK:].astype(BF16)
        else:
            out[...] = value.astype(out.dtype)


def split_over_x(pos, mine, received, p0, p1, p2, p3):
    for k, out in enumerate((p0, p1, p2, p3)):
        rows = pl.ds(lax.rem(pos[0] + k, X) * BLK, BLK)
        out[...] = (mine[rows, :] + received[rows, :].astype(F32)).astype(out.dtype)


def split_over_zh(pos, own, r1, r2, r3, p0, p1, p2, p3):
    for k, out in enumerate((p0, p1, p2, p3)):
        rows = pl.ds(lax.rem(pos[1] + k, ZH) * 32, 32)
        total = own[rows, :]
        for r in (r1, r2, r3):
            total = total + r[rows, :].astype(F32)
        out[...] = total.astype(out.dtype)


def add_passing(o1, o3, passing1, passing3, out1, out3):
    out1[:BLK, :] = (o1[:BLK, :].astype(F32) + passing1[...].astype(F32)).astype(BF16)
    out1[BLK:, :] = o1[BLK:, :]
    out3[:BLK, :] = o3[:BLK, :]
    out3[BLK:, :] = (o3[BLK:, :].astype(F32) + passing3[...].astype(F32)).astype(BF16)


def split_over_zl(pos, own, r1, r3, keep, give):
    zl = pos[2]
    for out, half in ((give, 1 - zl), (keep, zl)):
        rows = pl.ds(half * BLK, BLK)
        out[...] = (own[rows, :] + r1[rows, :].astype(F32) + r3[rows, :].astype(F32)).astype(out.dtype)


def shape(dims, dtype=F32):
    return jax.ShapeDtypeStruct(dims, dtype)


VEC = (TILES, BLK)
ROWS = pltpu.VMEM((SIDE, BLK), F32)


def run(kernel, outs, scratch, smem, *args, limit=6):
    return pl.pallas_call(
        kernel,
        out_shape=outs,
        in_specs=[SMEM] * smem + [VMEM] * (len(args) - smem),
        out_specs=[VMEM] * len(outs),
        scratch_shapes=scratch,
        compiler_params=pltpu.CompilerParams(vmem_limit_bytes=limit * MIB),
    )(*args)


def ring(n, k):
    return [(i, (i + k) % n) for i in range(n)]


def over_txt(v):
    return lax.all_to_all(v, ("y", "zl"), 0, 0, tiled=True)


def over_img(v):
    return lax.all_to_all(v, ("x", "zh", "c"), 0, 0, tiled=True)


def over_img2(v):
    both = v + lax.ppermute(v, "c", ring(C, 1))
    return lax.all_to_all(jnp.broadcast_to(both, (N_IMG // C,) + v.shape[1:]), ("x", "zh"), 0, 0, tiled=True)


def over_img_stats(v):
    other = lax.ppermute(v, "c", ring(C, 1))
    top = jnp.maximum(v[0, 0], other[0, 0])
    total = v[0, 1] * jnp.exp(v[0, 0] - top) + other[0, 1] * jnp.exp(other[0, 0] - top)
    both = jnp.stack([top, total])
    return lax.all_to_all(jnp.broadcast_to(both, (N_IMG // C,) + v.shape[1:]), ("x", "zh"), 0, 0, tiled=True)


def on_device(images, captions, tile_mask):
    pos = jnp.stack([lax.axis_index(name) for name in ("x", "zh", "zl", "y", "c")]).astype(jnp.int32)
    swap = ring(2, 1)
    sibling = lax.ppermute(images, "zl", swap)
    z1, z2, z3 = (lax.ppermute(captions, "zh", ring(ZH, k)) for k in (1, 2, 3))
    m10 = lax.ppermute(tile_mask, "zl", swap)
    sibling, z1, z2, z3, m10 = lax.optimization_barrier((sibling, z1, z2, z3, m10))
    m01 = lax.ppermute(tile_mask, "c", swap)
    m11 = lax.ppermute(m10, "c", swap)
    cap_z = jnp.stack([captions, z1, z2, z3])
    i0 = jnp.stack([images, sibling])
    i1, i3 = (lax.ppermute(i0, "y", ring(Y, k)) for k in (1, 3))
    c1, c2, c3 = (lax.ppermute(cap_z, "x", ring(X, k)) for k in (1, 2, 3))
    i1, i3, c1, c3 = lax.optimization_barrier((i1, i3, c1, c3))
    i2 = lax.ppermute(i1, "y", ring(Y, 1))
    caps = [cap_z, c1, c2, c3]
    other_caps = [lax.ppermute(piece, "c", swap) for piece in caps]

    to_txt = shape((N_TXT, 1) + VEC)
    to_img = shape((N_IMG, 1) + VEC)
    square = (SIDE, SIDE)
    img, cap, s, row_stats, mask = run(
        scores_kernel,
        [shape(square, BF16), shape(square, BF16), shape(square), shape((N_TXT, 2) + VEC), shape((TILES * TILES, BLK))],
        [], 5, pos, tile_mask, m01, m10, m11, i0, i1, i2, i3, *caps, *other_caps, limit=10,
    )
    e, col_stats, top = run(
        kernel_matrix, [shape(square), shape((1, 2) + VEC), shape(VEC)],
        [pltpu.VMEM(VEC, F32), ROWS], 0, mask, over_txt(row_stats), s,
    )
    x, f, fb0 = run(first_row_pass, [to_txt, shape(VEC), shape(VEC)], [], 0, over_img_stats(col_stats), top, e)
    y, a2 = run(col_pass, [to_img, shape(VEC)], [ROWS], 0, over_txt(x), f, e)
    vec = pltpu.VMEM(VEC, F32)
    x, b2 = run(row_pass, [to_txt, shape(VEC)], [vec], 0, over_img(y), f, e)
    y, a3 = run(last_col_pass, [shape((1, 2) + VEC), shape(VEC)], [ROWS], 0, over_txt(x), f, e, s)
    x, b3, gv3 = run(gu3_pass, [to_txt, shape(VEC), shape(VEC)], [vec, vec], 0, over_img2(y), f, a3, e, s)
    y, agu3 = run(functools.partial(gv_pass, scale=1.0), [to_img, shape(VEC)], [ROWS], 0, over_txt(x), a3, f, b2, e)
    x, bgv2 = run(gu_pass, [to_txt, shape(VEC)], [vec], 0, over_img(y), f, b2, e)
    one = jnp.ones(VEC, F32)
    y, agu2 = run(functools.partial(gv_pass, scale=1.0 / RATIO), [to_img, shape(VEC)], [ROWS], 0, over_txt(x), a2, f, one, e)
    x, gv1 = run(gu_pass, [to_txt, shape(VEC)], [vec], 0, over_img(y), f, one, e)
    gs, mine, other = run(
        captions_kernel, [shape(square, BF16), shape((512, SIDE)), shape((512, SIDE), BF16)],
        [vec] + [ROWS] * 5, 1,
        pos, over_txt(x), a2, a3, agu2, agu3, f, fb0, b2, b3, gv3, bgv2, gv1, e, s, img, limit=10,
    )
    other = lax.ppermute(other, "c", swap)
    block, half, part = (2 * BLK, SIDE), (BLK, SIDE), (32, SIDE)
    o0, o1, o3, o2a, o2b = run(
        images_kernel, [shape(block)] + [shape(block, BF16)] * 2 + [shape(half, BF16)] * 2,
        [], 1, pos, gs, cap, limit=10,
    )
    o2a = lax.ppermute(o2a, "y", ring(Y, 1))
    o2b = lax.ppermute(o2b, "y", ring(Y, 3))
    p0, p1, p2, p3 = run(split_over_x, [shape(half)] + [shape(half, BF16)] * 3, [], 1, pos, mine, other)
    p1, p2, p3 = (lax.ppermute(p, "x", ring(X, k)) for k, p in enumerate((p1, p2, p3), 1))
    o2a, o2b, p1, p2, p3 = lax.optimization_barrier((o2a, o2b, p1, p2, p3))
    o1, o3 = run(add_passing, [shape(block, BF16)] * 2, [], 0, o1, o3, o2a, o2b)
    o1 = lax.ppermute(o1, "y", ring(Y, 1))
    o3 = lax.ppermute(o3, "y", ring(Y, 3))
    q0, q1, q2, q3 = run(split_over_zh, [shape(part)] + [shape(part, BF16)] * 3, [], 1, pos, p0, p1, p2, p3)
    q1, q2, q3 = (lax.ppermute(q, "zh", ring(ZH, k)) for k, q in enumerate((q1, q2, q3), 1))
    keep, give = run(split_over_zl, [shape(half), shape(half, BF16)], [], 1, pos, o0, o1, o3)
    images_grad = keep + lax.ppermute(give, "zl", swap).astype(F32)
    captions_grad = q0 + q1.astype(F32) + q2.astype(F32) + q3.astype(F32)
    return (images_grad, captions_grad)


def solution(mesh):
    split = Mesh(mesh.devices.reshape(X, ZH, ZL, Y, C), ("x", "zh", "zl", "y", "c"))
    img, txt = ("x", "zh", "zl"), ("y", "c")
    in_specs = (P(img + txt, None), P(txt + img, None), P(img, txt))
    out_specs = (P(img + txt, None), P(txt + img, None))
    return jax.shard_map(on_device, mesh=split, in_specs=in_specs, out_specs=out_specs, check_vma=False)
```

```python
import functools

import jax
import jax.numpy as jnp
from jax import lax
from jax.experimental import pallas as pl
from jax.experimental.pallas import tpu as pltpu
from jax.sharding import Mesh, PartitionSpec as P

BLK = 128
INVERSE_EPSILON = 4.0
NEG = -1e30
X, ZH, ZL, Y, C = 4, 4, 2, 4, 2
N_IMG, N_TXT = X * ZH * C, Y * ZL
TILES = 8
SIDE = TILES * BLK
F32, BF16 = jnp.float32, jnp.bfloat16
RATIO = 4.0

VMEM = pl.BlockSpec(memory_space=pltpu.VMEM)
SMEM = pl.BlockSpec(memory_space=pltpu.SMEM)
MIB = 1024 * 1024


def tile(index):
    return pl.ds(index * BLK, BLK)


def spread_rows(vec_ref, out_ref):
    for q in range(TILES):
        row = jnp.broadcast_to(vec_ref[q : q + 1, :], (BLK, BLK))
        out_ref[tile(q), :] = row.T


def put_all(out_ref, slot, q, row):
    for peer in range(out_ref.shape[0]):
        out_ref[peer, slot, q : q + 1, :] = row


def row_totals(out_ref, slot, term):
    for q in range(TILES):
        total = term(q, 0)
        for t in range(1, TILES):
            total = total + term(q, t)
        put_all(out_ref, slot, q, jnp.sum(total.T, axis=0, keepdims=True))


def col_totals(out_ref, slot, term, scale):
    for t in range(TILES):
        total = term(0, t)
        for q in range(1, TILES):
            total = total + term(q, t)
        put_all(out_ref, slot, t, jnp.sum(total, axis=0, keepdims=True) * scale[t : t + 1, :])


def log_sum(top, total):
    return jnp.where(top > NEG, top + jnp.log(total), NEG)


def kept(mask, q, t):
    return jnp.broadcast_to(mask[q * TILES + t : q * TILES + t + 1, :], (BLK, BLK)) > 0


def spread_mask(pos, m00, m01, m10, m11, mask):
    zl, c = pos[2], pos[4]
    left = lax.broadcasted_iota(jnp.int32, (1, BLK), 1) < BLK // 2
    for y in range(Y):
        for dz in range(ZL):
            row = y * 2 + c
            q = y * 2 + jnp.where(dz == 0, zl, 1 - zl)
            for dc, flags in enumerate((m10, m11) if dz else (m00, m01)):
                column = jnp.where(dc == 0, c, 1 - c)
                for x in range(X):
                    lanes = jnp.where(left, flags[row, 2 * x], flags[row, 2 * x + 1])
                    mask[pl.ds(q * TILES + column * X + x, 1), :] = lanes.astype(F32)


def place_images(pos, pieces, k, img):
    source = lax.rem(pos[3] - k + Y, Y)
    for slot in range(2):
        half = jnp.where(slot == 0, pos[2], 1 - pos[2])
        img[pl.ds((source * 2 + half) * BLK, BLK), :] = pieces[slot]
    return source


def score_rows(source, mask, img, cap, s, stats):
    rows = pl.ds(pl.multiple_of(source * 256, 256), 256)
    s[rows, :] = lax.dot_general(
        img[rows, :], cap[...], (((1,), (1,)), ((), ())), preferred_element_type=F32
    )
    for j in range(2):
        q = source * 2 + j
        rows = pl.ds(pl.multiple_of(q * BLK, BLK), BLK)

        def block(t):
            keep = jnp.broadcast_to(mask[pl.ds(q * TILES + t, 1), :], (BLK, BLK)) > 0
            return jnp.where(keep, s[rows, tile(t)] * INVERSE_EPSILON, NEG)

        top = block(0)
        for t in range(1, TILES):
            top = jnp.maximum(top, block(t))
        top_col = jnp.max(top, axis=1, keepdims=True)
        total = jnp.zeros((BLK, BLK), F32)
        for t in range(TILES):
            total = total + jnp.exp(block(t) - top_col)
        value = log_sum(jnp.max(top.T, axis=0, keepdims=True), jnp.sum(total.T, axis=0, keepdims=True))
        for peer in range(N_TXT):
            stats[peer, 0, pl.ds(q, 1), :] = value


def scores_kernel(
    pos, m00, m01, m10, m11, i0, i1, i3, c0, c1, c2, c3, d0, d1, d2, d3, img, cap, s, stats, mask
):
    x, zh, c = pos[0], pos[1], pos[4]
    spread_mask(pos, m00, m01, m10, m11, mask)
    for k, (own, other) in enumerate(((c0, d0), (c1, d1), (c2, d2), (c3, d3))):
        source = lax.rem(x - k + X, X)
        for j in range(ZH):
            place = lax.rem(zh - j + ZH, ZH) * 32
            cap[pl.ds((c * X + source) * BLK + place, 32), :] = own[j]
            cap[pl.ds(((1 - c) * X + source) * BLK + place, 32), :] = other[j]
    for k, pieces in ((0, i0), (1, i1), (3, i3)):
        source = place_images(pos, pieces, k, img)
        score_rows(source, mask, img, cap, s, stats)


def last_scores_kernel(pos, i2, cap, mask, img_in, s_in, stats_in, img, s, stats):
    source = place_images(pos, i2, 2, img)
    score_rows(source, mask, img, cap, s, stats)


def joined(stats):
    top = jnp.max(stats[:, 0], axis=0)
    return top, jnp.sum(jnp.exp(stats[:, 0] - top[None]), axis=0)


def kernel_matrix(mask, row_stats, s, e, stats, top_out, u_vec, u_rows):
    top, total = joined(row_stats)
    u_vec[...] = -(top + jnp.log(total))
    spread_rows(u_vec, u_rows)
    for t in range(TILES):
        top = jnp.full((BLK, BLK), NEG, F32)
        for q in range(TILES):
            w = s[tile(q), tile(t)] * INVERSE_EPSILON + u_rows[tile(q), :]
            top = jnp.maximum(top, jnp.where(kept(mask, q, t), w, NEG))
        top_row = jnp.max(top, axis=0, keepdims=True)
        total = jnp.zeros((BLK, BLK), F32)
        for q in range(TILES):
            w = s[tile(q), tile(t)] * INVERSE_EPSILON + u_rows[tile(q), :]
            keep = kept(mask, q, t)
            value = jnp.where(keep, jnp.exp(jnp.where(keep, w, NEG) - top_row), 0.0)
            e[tile(q), tile(t)] = value
            total = total + value
        top_out[t : t + 1, :] = top_row
        put_all(stats, 0, t, log_sum(top_row, jnp.sum(total, axis=0, keepdims=True)))


def first_row_pass(col_stats, own_top, e, x, f, fb0):
    top, total = joined(col_stats)
    mine = own_top[...]
    f[...] = RATIO * jnp.exp(mine - top) / total
    fb0[...] = jnp.exp(mine)
    row_totals(x, 0, lambda q, t: e[tile(q), tile(t)] * f[t : t + 1, :])


def col_pass(x_all, f, e, y, a, rows):
    a[...] = 1.0 / jnp.sum(x_all[:, 0], axis=0)
    spread_rows(a, rows)
    col_totals(y, 0, lambda q, t: e[tile(q), tile(t)] * rows[tile(q), :], f[...])


def row_pass(y_all, f, e, x, b, fb):
    b[...] = RATIO / jnp.sum(y_all[:, 0], axis=0)
    fb[...] = f[...] * b[...]
    row_totals(x, 0, lambda q, t: e[tile(q), tile(t)] * fb[t : t + 1, :])


def last_col_pass(x_all, f, e, s, y, a, rows):
    a[...] = 1.0 / jnp.sum(x_all[:, 0], axis=0)
    spread_rows(a, rows)
    scale = f[...]
    for t in range(TILES):
        total = jnp.zeros((BLK, BLK), F32)
        scored = jnp.zeros((BLK, BLK), F32)
        for q in range(TILES):
            value = e[tile(q), tile(t)] * rows[tile(q), :]
            total = total + value
            scored = scored + value * s[tile(q), tile(t)]
        put_all(y, 0, t, jnp.sum(total, axis=0, keepdims=True) * scale[t : t + 1, :])
        put_all(y, 1, t, jnp.sum(scored, axis=0, keepdims=True) * scale[t : t + 1, :])


def gu3_pass(y_all, f, a3, e, s, x, b3, gv3, c0, c1):
    b3[...] = RATIO / jnp.sum(y_all[:, 0], axis=0)
    gv3[...] = -b3[...] * jnp.sum(y_all[:, 1], axis=0)
    c1[...] = f[...] * b3[...]
    c0[...] = c1[...] * gv3[...] * (1.0 / RATIO)
    row_totals(
        x, 0, lambda q, t: e[tile(q), tile(t)] * (s[tile(q), tile(t)] * c1[t : t + 1, :] + c0[t : t + 1, :])
    )


def gv_pass(x_all, a, f, b, e, y, agu, rows, *, scale):
    gu = -scale * a[...] * jnp.sum(x_all[:, 0], axis=0)
    agu[...] = a[...] * gu
    spread_rows(agu, rows)
    col_totals(y, 0, lambda q, t: e[tile(q), tile(t)] * rows[tile(q), :], -(f[...] * b[...]))


def gu_pass(y_all, f, b, e, x, bgv, c):
    bgv[...] = b[...] * jnp.sum(y_all[:, 0], axis=0)
    c[...] = f[...] * bgv[...]
    row_totals(x, 0, lambda q, t: e[tile(q), tile(t)] * c[t : t + 1, :])


def captions_kernel(
    pos, x_all, a2, a3, agu2, agu3, f, fb0, b2, b3, gv3, bgv2, gv1, e, s, img,
    gs, mine, other, vec, r_a3, r_a2, r_gu3, r_gu2, r_gu1,
):
    spread_rows(a3, r_a3)
    spread_rows(a2, r_a2)
    vec[...] = INVERSE_EPSILON * agu3[...]
    spread_rows(vec, r_gu3)
    vec[...] = INVERSE_EPSILON * agu2[...]
    spread_rows(vec, r_gu2)
    vec[...] = (-INVERSE_EPSILON / RATIO) * jnp.sum(x_all[:, 0], axis=0)
    spread_rows(vec, r_gu1)
    scale = f[...]
    k_s = -INVERSE_EPSILON * (scale * b3[...])
    k_a3 = -(scale * b3[...]) * (1.0 + gv3[...])
    k_a2 = -scale * bgv2[...]
    k_1 = -scale * gv1[...]
    k_gu3 = -scale * b2[...]
    k_gu2 = -scale
    k_gu1 = -fb0[...]
    for t in range(TILES):
        pick = slice(t, t + 1)
        for q in range(TILES):
            rows = tile(q)
            value = (
                r_a3[rows, :] * (k_a3[pick, :] + k_s[pick, :] * s[rows, tile(t)])
                + r_a2[rows, :] * k_a2[pick, :]
                + k_1[pick, :]
                + r_gu3[rows, :] * k_gu3[pick, :]
                + r_gu2[rows, :] * k_gu2[pick, :]
                + r_gu1[rows, :] * k_gu1[pick, :]
            )
            gs[rows, tile(t)] = (value * e[rows, tile(t)]).astype(BF16)
    core = pos[4]
    for out, c in ((other, 1 - core), (mine, core)):
        for half in range(2):
            columns = pl.ds(pl.multiple_of(c * 512 + half * 256, 256), 256)
            out[half * 256 : half * 256 + 256, :] = lax.dot_general(
                gs[:, columns], img[...], (((0,), (0,)), ((), ())), preferred_element_type=F32
            ).astype(out.dtype)


def images_kernel(pos, gs, cap, o0, o1, o3, o2a, o2b):
    y = pos[3]
    for k, out in ((2, None), (1, o1), (3, o3), (0, o0)):
        target = lax.rem(y + k, Y)
        value = jnp.dot(gs[pl.ds(target * 256, 256), :], cap[...], preferred_element_type=F32)
        if k == 2:
            o2a[...] = value[:BLK].astype(BF16)
            o2b[...] = value[BLK:].astype(BF16)
        else:
            out[...] = value.astype(out.dtype)


def split_over_x(pos, mine, received, p0, p1, p2, p3):
    for k, out in enumerate((p0, p1, p2, p3)):
        rows = pl.ds(lax.rem(pos[0] + k, X) * BLK, BLK)
        out[...] = (mine[rows, :] + received[rows, :].astype(F32)).astype(out.dtype)


def split_over_zh(pos, own, r1, r2, r3, p0, p1, p2, p3):
    for k, out in enumerate((p0, p1, p2, p3)):
        rows = pl.ds(lax.rem(pos[1] + k, ZH) * 32, 32)
        total = own[rows, :]
        for r in (r1, r2, r3):
            total = total + r[rows, :].astype(F32)
        out[...] = total.astype(out.dtype)


def add_passing(o1, o3, passing1, passing3, out1, out3):
    out1[:BLK, :] = (o1[:BLK, :].astype(F32) + passing1[...].astype(F32)).astype(BF16)
    out1[BLK:, :] = o1[BLK:, :]
    out3[:BLK, :] = o3[:BLK, :]
    out3[BLK:, :] = (o3[BLK:, :].astype(F32) + passing3[...].astype(F32)).astype(BF16)


def split_over_zl(pos, own, r1, r3, keep, give):
    zl = pos[2]
    for out, half in ((give, 1 - zl), (keep, zl)):
        rows = pl.ds(half * BLK, BLK)
        out[...] = (own[rows, :] + r1[rows, :].astype(F32) + r3[rows, :].astype(F32)).astype(out.dtype)


def shape(dims, dtype=F32):
    return jax.ShapeDtypeStruct(dims, dtype)


VEC = (TILES, BLK)
ROWS = pltpu.VMEM((SIDE, BLK), F32)


def run(kernel, outs, scratch, smem, *args, limit=6, aliases={}):
    return pl.pallas_call(
        kernel,
        out_shape=outs,
        in_specs=[SMEM] * smem + [VMEM] * (len(args) - smem),
        out_specs=[VMEM] * len(outs),
        scratch_shapes=scratch,
        input_output_aliases=aliases,
        compiler_params=pltpu.CompilerParams(vmem_limit_bytes=limit * MIB),
    )(*args)


def ring(n, k):
    return [(i, (i + k) % n) for i in range(n)]


def over_txt(v):
    return lax.all_to_all(v, ("y", "zl"), 0, 0, tiled=True)


def over_img(v):
    return lax.all_to_all(v, ("x", "zh", "c"), 0, 0, tiled=True)


def over_img2(v):
    both = v + lax.ppermute(v, "c", ring(C, 1))
    return lax.all_to_all(jnp.broadcast_to(both, (N_IMG // C,) + v.shape[1:]), ("x", "zh"), 0, 0, tiled=True)


def on_device(images, captions, tile_mask):
    pos = jnp.stack([lax.axis_index(name) for name in ("x", "zh", "zl", "y", "c")]).astype(jnp.int32)
    swap = ring(2, 1)
    sibling = lax.ppermute(images, "zl", swap)
    z1, z2, z3 = (lax.ppermute(captions, "zh", ring(ZH, k)) for k in (1, 2, 3))
    m10 = lax.ppermute(tile_mask, "zl", swap)
    m00 = jnp.minimum(tile_mask, 1)
    sibling, z1, z2, z3, m00, m10 = lax.optimization_barrier((sibling, z1, z2, z3, m00, m10))
    m01 = lax.ppermute(tile_mask, "c", swap)
    m11 = lax.ppermute(m10, "c", swap)
    cap_z = jnp.stack([captions, z1, z2, z3])
    i0 = jnp.stack([images, sibling])
    i1, i3 = (lax.ppermute(i0, "y", ring(Y, k)) for k in (1, 3))
    c1, c2, c3 = (lax.ppermute(cap_z, "x", ring(X, k)) for k in (1, 2, 3))
    i1, i3, c1, c3 = lax.optimization_barrier((i1, i3, c1, c3))
    i2 = lax.ppermute(i1, "y", ring(Y, 1))
    caps = [cap_z, c1, c2, c3]
    other_caps = [lax.ppermute(piece, "c", swap) for piece in caps]

    to_txt = shape((N_TXT, 1) + VEC)
    to_img = shape((N_IMG, 1) + VEC)
    square = (SIDE, SIDE)
    img, cap, s, row_stats, mask = run(
        scores_kernel,
        [shape(square, BF16), shape(square, BF16), shape(square), to_txt, shape((TILES * TILES, BLK))],
        [], 5, pos, m00, m01, m10, m11, i0, i1, i3, *caps, *other_caps, limit=10,
    )
    img, s, row_stats = run(
        last_scores_kernel, [shape(square, BF16), shape(square), to_txt],
        [], 1, pos, i2, cap, mask, img, s, row_stats, limit=10, aliases={4: 0, 5: 1, 6: 2},
    )
    e, col_stats, top = run(
        kernel_matrix, [shape(square), to_img, shape(VEC)],
        [pltpu.VMEM(VEC, F32), ROWS], 0, mask, over_txt(row_stats), s,
    )
    x, f, fb0 = run(first_row_pass, [to_txt, shape(VEC), shape(VEC)], [], 0, over_img(col_stats), top, e)
    y, a2 = run(col_pass, [to_img, shape(VEC)], [ROWS], 0, over_txt(x), f, e)
    vec = pltpu.VMEM(VEC, F32)
    x, b2 = run(row_pass, [to_txt, shape(VEC)], [vec], 0, over_img(y), f, e)
    y, a3 = run(last_col_pass, [shape((1, 2) + VEC), shape(VEC)], [ROWS], 0, over_txt(x), f, e, s)
    x, b3, gv3 = run(gu3_pass, [to_txt, shape(VEC), shape(VEC)], [vec, vec], 0, over_img2(y), f, a3, e, s)
    y, agu3 = run(functools.partial(gv_pass, scale=1.0), [to_img, shape(VEC)], [ROWS], 0, over_txt(x), a3, f, b2, e)
    x, bgv2 = run(gu_pass, [to_txt, shape(VEC)], [vec], 0, over_img(y), f, b2, e)
    one = jnp.ones(VEC, F32)
    y, agu2 = run(functools.partial(gv_pass, scale=1.0 / RATIO), [to_img, shape(VEC)], [ROWS], 0, over_txt(x), a2, f, one, e)
    x, gv1 = run(gu_pass, [to_txt, shape(VEC)], [vec], 0, over_img(y), f, one, e)
    gs, mine, other = run(
        captions_kernel, [shape(square, BF16), shape((512, SIDE)), shape((512, SIDE), BF16)],
        [vec] + [ROWS] * 5, 1,
        pos, over_txt(x), a2, a3, agu2, agu3, f, fb0, b2, b3, gv3, bgv2, gv1, e, s, img, limit=10,
    )
    other = lax.ppermute(other, "c", swap)
    block, half, part = (2 * BLK, SIDE), (BLK, SIDE), (32, SIDE)
    o0, o1, o3, o2a, o2b = run(
        images_kernel, [shape(block)] + [shape(block, BF16)] * 2 + [shape(half, BF16)] * 2,
        [], 1, pos, gs, cap, limit=10,
    )
    o2a = lax.ppermute(o2a, "y", ring(Y, 1))
    o2b = lax.ppermute(o2b, "y", ring(Y, 3))
    p0, p1, p2, p3 = run(split_over_x, [shape(half)] + [shape(half, BF16)] * 3, [], 1, pos, mine, other)
    p1, p2, p3 = (lax.ppermute(p, "x", ring(X, k)) for k, p in enumerate((p1, p2, p3), 1))
    o2a, o2b, p1, p3 = lax.optimization_barrier((o2a, o2b, p1, p3))
    o1, o3 = run(add_passing, [shape(block, BF16)] * 2, [], 0, o1, o3, o2a, o2b)
    o1 = lax.ppermute(o1, "y", ring(Y, 1))
    o3 = lax.ppermute(o3, "y", ring(Y, 3))
    q0, q1, q2, q3 = run(split_over_zh, [shape(part)] + [shape(part, BF16)] * 3, [], 1, pos, p0, p1, p2, p3)
    q1, q2, q3 = (lax.ppermute(q, "zh", ring(ZH, k)) for k, q in enumerate((q1, q2, q3), 1))
    keep, give = run(split_over_zl, [shape(half), shape(half, BF16)], [], 1, pos, o0, o1, o3)
    images_grad = keep + lax.ppermute(give, "zl", swap).astype(F32)
    captions_grad = q0 + q1.astype(F32) + q2.astype(F32) + q3.astype(F32)
    return (images_grad, captions_grad)


def solution(mesh):
    split = Mesh(mesh.devices.reshape(X, ZH, ZL, Y, C), ("x", "zh", "zl", "y", "c"))
    img, txt = ("x", "zh", "zl"), ("y", "c")
    in_specs = (P(img + txt, None), P(txt + img, None), P(img, txt))
    out_specs = (P(img + txt, None), P(txt + img, None))
    return jax.shard_map(on_device, mesh=split, in_specs=in_specs, out_specs=out_specs, check_vma=False)
```

```python
import functools

import jax
import jax.numpy as jnp
from jax import lax
from jax.experimental import pallas as pl
from jax.experimental.pallas import tpu as pltpu
from jax.sharding import Mesh, PartitionSpec as P

BLK = 128
INVERSE_EPSILON = 4.0
NEG = -1e30
X, ZH, ZL, Y, C = 4, 4, 2, 4, 2
N_IMG, N_TXT = X * ZH * C, Y * ZL
TILES = 8
SIDE = TILES * BLK
F32, BF16 = jnp.float32, jnp.bfloat16
RATIO = 4.0

VMEM = pl.BlockSpec(memory_space=pltpu.VMEM)
SMEM = pl.BlockSpec(memory_space=pltpu.SMEM)
MIB = 1024 * 1024


def tile(index):
    return pl.ds(index * BLK, BLK)


def spread_rows(vec_ref, out_ref):
    for q in range(TILES):
        row = jnp.broadcast_to(vec_ref[q : q + 1, :], (BLK, BLK))
        out_ref[tile(q), :] = row.T


def put_all(out_ref, slot, q, row):
    for peer in range(out_ref.shape[0]):
        out_ref[peer, slot, q : q + 1, :] = row


def row_totals(out_ref, slot, term):
    for q in range(TILES):
        total = term(q, 0)
        for t in range(1, TILES):
            total = total + term(q, t)
        put_all(out_ref, slot, q, jnp.sum(total.T, axis=0, keepdims=True))


def col_totals(out_ref, slot, term, scale):
    for t in range(TILES):
        total = term(0, t)
        for q in range(1, TILES):
            total = total + term(q, t)
        put_all(out_ref, slot, t, jnp.sum(total, axis=0, keepdims=True) * scale[t : t + 1, :])


def log_sum(top, total):
    return jnp.where(top > NEG, top + jnp.log(total), NEG)


def kept(mask, q, t):
    return jnp.broadcast_to(mask[q * TILES + t : q * TILES + t + 1, :], (BLK, BLK)) > 0


def spread_mask(pos, m00, m01, m10, m11, mask):
    zl, c = pos[2], pos[4]
    left = lax.broadcasted_iota(jnp.int32, (1, BLK), 1) < BLK // 2
    for y in range(Y):
        for dz in range(ZL):
            row = y * 2 + c
            q = y * 2 + jnp.where(dz == 0, zl, 1 - zl)
            for dc, flags in enumerate((m10, m11) if dz else (m00, m01)):
                column = jnp.where(dc == 0, c, 1 - c)
                for x in range(X):
                    lanes = jnp.where(left, flags[row, 2 * x], flags[row, 2 * x + 1])
                    mask[pl.ds(q * TILES + column * X + x, 1), :] = lanes.astype(F32)


def place_images(pos, pieces, k, img):
    source = lax.rem(pos[3] - k + Y, Y)
    for slot in range(2):
        half = jnp.where(slot == 0, pos[2], 1 - pos[2])
        img[pl.ds((source * 2 + half) * BLK, BLK), :] = pieces[slot]
    return source


def score_rows(source, mask, img, cap, s, stats):
    rows = pl.ds(pl.multiple_of(source * 256, 256), 256)
    s[rows, :] = lax.dot_general(
        img[rows, :], cap[...], (((1,), (1,)), ((), ())), preferred_element_type=F32
    )
    for j in range(2):
        q = source * 2 + j
        rows = pl.ds(pl.multiple_of(q * BLK, BLK), BLK)

        def block(t):
            keep = jnp.broadcast_to(mask[pl.ds(q * TILES + t, 1), :], (BLK, BLK)) > 0
            return jnp.where(keep, s[rows, tile(t)] * INVERSE_EPSILON, NEG)

        top = block(0)
        for t in range(1, TILES):
            top = jnp.maximum(top, block(t))
        top_col = jnp.max(top, axis=1, keepdims=True)
        total = jnp.zeros((BLK, BLK), F32)
        for t in range(TILES):
            total = total + jnp.exp(block(t) - top_col)
        value = log_sum(jnp.max(top.T, axis=0, keepdims=True), jnp.sum(total.T, axis=0, keepdims=True))
        for peer in range(N_TXT):
            stats[peer, 0, pl.ds(q, 1), :] = value


def scores_kernel(
    pos, m00, m01, m10, m11, i0, i1, i3, c0, c1, c2, c3, d0, d1, d2, d3, img, cap, s, stats, mask
):
    x, zh, c = pos[0], pos[1], pos[4]
    spread_mask(pos, m00, m01, m10, m11, mask)
    for k, (own, other) in enumerate(((c0, d0), (c1, d1), (c2, d2), (c3, d3))):
        source = lax.rem(x - k + X, X)
        for j in range(ZH):
            place = lax.rem(zh - j + ZH, ZH) * 32
            cap[pl.ds((c * X + source) * BLK + place, 32), :] = own[j]
            cap[pl.ds(((1 - c) * X + source) * BLK + place, 32), :] = other[j]
    for k, pieces in ((0, i0), (1, i1), (3, i3)):
        source = place_images(pos, pieces, k, img)
        score_rows(source, mask, img, cap, s, stats)


def last_scores_kernel(pos, i2, cap, mask, img_in, s_in, stats_in, img, s, stats):
    source = place_images(pos, i2, 2, img)
    score_rows(source, mask, img, cap, s, stats)


def joined(stats):
    top = jnp.max(stats[:, 0], axis=0)
    return top, jnp.sum(jnp.exp(stats[:, 0] - top[None]), axis=0)


def kernel_matrix(mask, row_stats, s, e, stats, top_out, u_vec, u_rows):
    top, total = joined(row_stats)
    u_vec[...] = -(top + jnp.log(total))
    spread_rows(u_vec, u_rows)
    for t in range(TILES):
        def masked(q):
            rows = pl.ds(pl.multiple_of(q * BLK, BLK), BLK)
            w = s[rows, tile(t)] * INVERSE_EPSILON + u_rows[rows, :]
            keep = jnp.broadcast_to(mask[pl.ds(q * TILES + t, 1), :], (BLK, BLK)) > 0
            return rows, keep, jnp.where(keep, w, NEG)

        top = lax.fori_loop(
            0, TILES, lambda q, top: jnp.maximum(top, masked(q)[2]), jnp.full((BLK, BLK), NEG, F32)
        )
        top_row = jnp.max(top, axis=0, keepdims=True)

        def fill(q, total):
            rows, keep, w = masked(q)
            value = jnp.where(keep, jnp.exp(w - top_row), 0.0)
            e[rows, tile(t)] = value
            return total + value

        total = lax.fori_loop(0, TILES, fill, jnp.zeros((BLK, BLK), F32))
        top_out[t : t + 1, :] = top_row
        put_all(stats, 0, t, log_sum(top_row, jnp.sum(total, axis=0, keepdims=True)))


def first_row_pass(col_stats, own_top, e, x, f, fb0):
    top, total = joined(col_stats)
    mine = own_top[...]
    f[...] = RATIO * jnp.exp(mine - top) / total
    fb0[...] = jnp.exp(mine)
    row_totals(x, 0, lambda q, t: e[tile(q), tile(t)] * f[t : t + 1, :])


def col_pass(x_all, f, e, y, a, rows):
    a[...] = 1.0 / jnp.sum(x_all[:, 0], axis=0)
    spread_rows(a, rows)
    col_totals(y, 0, lambda q, t: e[tile(q), tile(t)] * rows[tile(q), :], f[...])


def row_pass(y_all, f, e, x, b, fb):
    b[...] = RATIO / jnp.sum(y_all[:, 0], axis=0)
    fb[...] = f[...] * b[...]
    row_totals(x, 0, lambda q, t: e[tile(q), tile(t)] * fb[t : t + 1, :])


def last_col_pass(x_all, f, e, s, y, a, rows):
    a[...] = 1.0 / jnp.sum(x_all[:, 0], axis=0)
    spread_rows(a, rows)
    scale = f[...]
    for t in range(TILES):
        total = jnp.zeros((BLK, BLK), F32)
        scored = jnp.zeros((BLK, BLK), F32)
        for q in range(TILES):
            value = e[tile(q), tile(t)] * rows[tile(q), :]
            total = total + value
            scored = scored + value * s[tile(q), tile(t)]
        put_all(y, 0, t, jnp.sum(total, axis=0, keepdims=True) * scale[t : t + 1, :])
        put_all(y, 1, t, jnp.sum(scored, axis=0, keepdims=True) * scale[t : t + 1, :])


def gu3_pass(y_all, f, a3, e, s, x, b3, gv3, c0, c1):
    b3[...] = RATIO / jnp.sum(y_all[:, 0], axis=0)
    gv3[...] = -b3[...] * jnp.sum(y_all[:, 1], axis=0)
    c1[...] = f[...] * b3[...]
    c0[...] = c1[...] * gv3[...] * (1.0 / RATIO)
    row_totals(
        x, 0, lambda q, t: e[tile(q), tile(t)] * (s[tile(q), tile(t)] * c1[t : t + 1, :] + c0[t : t + 1, :])
    )


def gv_pass(x_all, a, f, b, e, y, rows, agu, *, scale):
    gu = -scale * a[...] * jnp.sum(x_all[:, 0], axis=0)
    agu[...] = a[...] * gu
    spread_rows(agu, rows)
    col_totals(y, 0, lambda q, t: e[tile(q), tile(t)] * rows[tile(q), :], -(f[...] * b[...]))


def gu_pass(y_all, f, b, e, x, bgv, c):
    bgv[...] = b[...] * jnp.sum(y_all[:, 0], axis=0)
    c[...] = f[...] * bgv[...]
    row_totals(x, 0, lambda q, t: e[tile(q), tile(t)] * c[t : t + 1, :])


def captions_kernel(
    pos, x_all, r_a2, r_a3, r_gu2, r_gu3, f, fb0, b2, b3, gv3, bgv2, gv1, e, s, img,
    gs, mine, other, vec, r_gu1,
):
    vec[...] = (-INVERSE_EPSILON / RATIO) * jnp.sum(x_all[:, 0], axis=0)
    spread_rows(vec, r_gu1)
    scale = f[...]
    k_s = -INVERSE_EPSILON * (scale * b3[...])
    k_a3 = -(scale * b3[...]) * (1.0 + gv3[...])
    k_a2 = -scale * bgv2[...]
    k_1 = -scale * gv1[...]
    k_gu3 = -INVERSE_EPSILON * (scale * b2[...])
    k_gu2 = -INVERSE_EPSILON * scale
    k_gu1 = -fb0[...]
    for t in range(TILES):
        pick = slice(t, t + 1)

        @pl.loop(0, TILES)
        def _(q):
            rows = pl.ds(pl.multiple_of(q * BLK, BLK), BLK)
            value = (
                r_a3[rows, :] * (k_a3[pick, :] + k_s[pick, :] * s[rows, tile(t)])
                + r_a2[rows, :] * k_a2[pick, :]
                + k_1[pick, :]
                + r_gu3[rows, :] * k_gu3[pick, :]
                + r_gu2[rows, :] * k_gu2[pick, :]
                + r_gu1[rows, :] * k_gu1[pick, :]
            )
            gs[rows, tile(t)] = (value * e[rows, tile(t)]).astype(BF16)

    core = pos[4]
    for out, c in ((other, 1 - core), (mine, core)):
        for half in range(2):
            columns = pl.ds(pl.multiple_of(c * 512 + half * 256, 256), 256)
            out[half * 256 : half * 256 + 256, :] = lax.dot_general(
                gs[:, columns], img[...], (((0,), (0,)), ((), ())), preferred_element_type=F32
            ).astype(out.dtype)


def images_kernel(pos, gs, cap, o0, o1, o3, o2a, o2b):
    y = pos[3]
    for k, out in ((2, None), (1, o1), (3, o3), (0, o0)):
        target = lax.rem(y + k, Y)
        value = jnp.dot(gs[pl.ds(target * 256, 256), :], cap[...], preferred_element_type=F32)
        if k == 2:
            o2a[...] = value[:BLK].astype(BF16)
            o2b[...] = value[BLK:].astype(BF16)
        else:
            out[...] = value.astype(out.dtype)


def split_over_x(pos, mine, received, p0, p1, p2, p3):
    for k, out in enumerate((p0, p1, p2, p3)):
        rows = pl.ds(lax.rem(pos[0] + k, X) * BLK, BLK)
        out[...] = (mine[rows, :] + received[rows, :].astype(F32)).astype(out.dtype)


def sum_over_x(own, r1, r2, r3, out):
    total = own[...]
    for r in (r1, r2, r3):
        total = total + r[...].astype(F32)
    out[...] = total.astype(BF16)


def add_passing(o1, o3, passing1, passing3, out1, out3):
    out1[:BLK, :] = (o1[:BLK, :].astype(F32) + passing1[...].astype(F32)).astype(BF16)
    out1[BLK:, :] = o1[BLK:, :]
    out3[:BLK, :] = o3[:BLK, :]
    out3[BLK:, :] = (o3[BLK:, :].astype(F32) + passing3[...].astype(F32)).astype(BF16)


def split_over_zl(pos, own, r1, r3, keep, give):
    zl = pos[2]
    for out, half in ((give, 1 - zl), (keep, zl)):
        rows = pl.ds(half * BLK, BLK)
        out[...] = (own[rows, :] + r1[rows, :].astype(F32) + r3[rows, :].astype(F32)).astype(out.dtype)


def shape(dims, dtype=F32):
    return jax.ShapeDtypeStruct(dims, dtype)


VEC = (TILES, BLK)
ROWS = pltpu.VMEM((SIDE, BLK), F32)
SPREAD = jax.ShapeDtypeStruct((SIDE, BLK), F32)


def run(kernel, outs, scratch, smem, *args, limit=6, aliases={}):
    return pl.pallas_call(
        kernel,
        out_shape=outs,
        in_specs=[SMEM] * smem + [VMEM] * (len(args) - smem),
        out_specs=[VMEM] * len(outs),
        scratch_shapes=scratch,
        input_output_aliases=aliases,
        compiler_params=pltpu.CompilerParams(vmem_limit_bytes=limit * MIB),
    )(*args)


def ring(n, k):
    return [(i, (i + k) % n) for i in range(n)]


def over_txt(v):
    return lax.all_to_all(v, ("y", "zl"), 0, 0, tiled=True)


def over_img(v):
    return lax.all_to_all(v, ("x", "zh", "c"), 0, 0, tiled=True)


def over_img2(v):
    both = v + lax.ppermute(v, "c", ring(C, 1))
    return lax.all_to_all(jnp.broadcast_to(both, (N_IMG // C,) + v.shape[1:]), ("x", "zh"), 0, 0, tiled=True)


def on_device(images, captions, tile_mask):
    pos = jnp.stack([lax.axis_index(name) for name in ("x", "zh", "zl", "y", "c")]).astype(jnp.int32)
    swap = ring(2, 1)
    sibling = lax.ppermute(images, "zl", swap)
    z1, z2, z3 = (lax.ppermute(captions, "zh", ring(ZH, k)) for k in (1, 2, 3))
    m10 = lax.ppermute(tile_mask, "zl", swap)
    m00 = jnp.minimum(tile_mask, 1)
    sibling, z1, z2, z3, m00, m10 = lax.optimization_barrier((sibling, z1, z2, z3, m00, m10))
    m01 = lax.ppermute(tile_mask, "c", swap)
    m11 = lax.ppermute(m10, "c", swap)
    cap_z = jnp.stack([captions, z1, z2, z3])
    c1, c2, c3 = (lax.ppermute(cap_z, "x", ring(X, k)) for k in (1, 2, 3))
    sibling, cap_z = lax.optimization_barrier((sibling, cap_z))
    i0 = jnp.stack([images, sibling])
    i1, i3 = (lax.ppermute(i0, "y", ring(Y, k)) for k in (1, 3))
    c1, c3, i1, i3 = lax.optimization_barrier((c1, c3, i1, i3))
    i2 = lax.ppermute(i1, "y", ring(Y, 1))
    caps = [cap_z, c1, c2, c3]
    other_caps = [lax.ppermute(piece, "c", swap) for piece in caps]

    to_txt = shape((N_TXT, 1) + VEC)
    to_img = shape((N_IMG, 1) + VEC)
    square = (SIDE, SIDE)
    img, cap, s, row_stats, mask = run(
        scores_kernel,
        [shape(square, BF16), shape(square, BF16), shape(square), to_txt, shape((TILES * TILES, BLK))],
        [], 5, pos, m00, m01, m10, m11, i0, i1, i3, *caps, *other_caps, limit=10,
    )
    img, s, row_stats = run(
        last_scores_kernel, [shape(square, BF16), shape(square), to_txt],
        [], 1, pos, i2, cap, mask, img, s, row_stats, limit=10, aliases={4: 0, 5: 1, 6: 2},
    )
    e, col_stats, top = run(
        kernel_matrix, [shape(square), to_img, shape(VEC)],
        [pltpu.VMEM(VEC, F32), ROWS], 0, mask, over_txt(row_stats), s,
    )
    x, f, fb0 = run(first_row_pass, [to_txt, shape(VEC), shape(VEC)], [], 0, over_img(col_stats), top, e)
    y, a2, r_a2 = run(col_pass, [to_img, shape(VEC), SPREAD], [], 0, over_txt(x), f, e)
    vec = pltpu.VMEM(VEC, F32)
    x, b2 = run(row_pass, [to_txt, shape(VEC)], [vec], 0, over_img(y), f, e)
    y, a3, r_a3 = run(last_col_pass, [shape((1, 2) + VEC), shape(VEC), SPREAD], [], 0, over_txt(x), f, e, s)
    x, b3, gv3 = run(gu3_pass, [to_txt, shape(VEC), shape(VEC)], [vec, vec], 0, over_img2(y), f, a3, e, s)
    y, r_gu3 = run(functools.partial(gv_pass, scale=1.0), [to_img, SPREAD], [vec], 0, over_txt(x), a3, f, b2, e)
    x, bgv2 = run(gu_pass, [to_txt, shape(VEC)], [vec], 0, over_img(y), f, b2, e)
    one = jnp.ones(VEC, F32)
    y, r_gu2 = run(functools.partial(gv_pass, scale=1.0 / RATIO), [to_img, SPREAD], [vec], 0, over_txt(x), a2, f, one, e)
    x, gv1 = run(gu_pass, [to_txt, shape(VEC)], [vec], 0, over_img(y), f, one, e)
    gs, mine, other = run(
        captions_kernel, [shape(square, BF16), shape((512, SIDE)), shape((512, SIDE), BF16)],
        [vec, ROWS], 1,
        pos, over_txt(x), r_a2, r_a3, r_gu2, r_gu3, f, fb0, b2, b3, gv3, bgv2, gv1, e, s, img, limit=10,
    )
    other = lax.ppermute(other, "c", swap)
    block, half, part = (2 * BLK, SIDE), (BLK, SIDE), (32, SIDE)
    o0, o1, o3, o2a, o2b = run(
        images_kernel, [shape(block)] + [shape(block, BF16)] * 2 + [shape(half, BF16)] * 2,
        [], 1, pos, gs, cap, limit=10,
    )
    o2a = lax.ppermute(o2a, "y", ring(Y, 1))
    o2b = lax.ppermute(o2b, "y", ring(Y, 3))
    p0, p1, p2, p3 = run(split_over_x, [shape(half)] + [shape(half, BF16)] * 3, [], 1, pos, mine, other)
    p1, p2, p3 = (lax.ppermute(p, "x", ring(X, k)) for k, p in enumerate((p1, p2, p3), 1))
    o2a, o2b, p1, p3 = lax.optimization_barrier((o2a, o2b, p1, p3))
    o1, o3 = run(add_passing, [shape(block, BF16)] * 2, [], 0, o1, o3, o2a, o2b)
    o1 = lax.ppermute(o1, "y", ring(Y, 1))
    o3 = lax.ppermute(o3, "y", ring(Y, 3))
    keep, give = run(split_over_zl, [shape(half), shape(half, BF16)], [], 1, pos, o0, o1, o3)
    images_grad = keep + lax.ppermute(give, "zl", swap).astype(F32)
    (q,) = run(sum_over_x, [shape(half, BF16)], [], 0, p0, p1, p2, p3)
    q = lax.all_to_all(q.reshape((ZH,) + part), "zh", 0, 0, tiled=True)
    captions_grad = jnp.sum(q.astype(F32), axis=0)
    return (images_grad, captions_grad)


def solution(mesh):
    split = Mesh(mesh.devices.reshape(X, ZH, ZL, Y, C), ("x", "zh", "zl", "y", "c"))
    img, txt = ("x", "zh", "zl"), ("y", "c")
    in_specs = (P(img + txt, None), P(txt + img, None), P(img, txt))
    out_specs = (P(img + txt, None), P(txt + img, None))
    return jax.shard_map(on_device, mesh=split, in_specs=in_specs, out_specs=out_specs, check_vma=False)
```

```python
import functools

import jax
import jax.numpy as jnp
from jax import lax
from jax.experimental import pallas as pl
from jax.experimental.pallas import tpu as pltpu
from jax.sharding import Mesh, PartitionSpec as P

BLK = 128
INVERSE_EPSILON = 4.0
NEG = -1e30
X, ZH, ZL, Y, C = 4, 4, 2, 4, 2
N_IMG, N_TXT = X * ZH * C, Y * ZL
TILES = 8
SIDE = TILES * BLK
F32, BF16 = jnp.float32, jnp.bfloat16
RATIO = 4.0

VMEM = pl.BlockSpec(memory_space=pltpu.VMEM)
SMEM = pl.BlockSpec(memory_space=pltpu.SMEM)
MIB = 1024 * 1024


def tile(index):
    return pl.ds(index * BLK, BLK)


def spread_rows(vec_ref, out_ref):
    for q in range(TILES):
        row = jnp.broadcast_to(vec_ref[q : q + 1, :], (BLK, BLK))
        out_ref[tile(q), :] = row.T


def put_all(out_ref, slot, q, row):
    for peer in range(out_ref.shape[0]):
        out_ref[peer, slot, q : q + 1, :] = row


def row_totals(out_ref, slot, term):
    for q in range(TILES):
        total = term(q, 0)
        for t in range(1, TILES):
            total = total + term(q, t)
        put_all(out_ref, slot, q, jnp.sum(total.T, axis=0, keepdims=True))


def col_totals(out_ref, slot, term, scale):
    for t in range(TILES):
        total = term(0, t)
        for q in range(1, TILES):
            total = total + term(q, t)
        put_all(out_ref, slot, t, jnp.sum(total, axis=0, keepdims=True) * scale[t : t + 1, :])


def log_sum(top, total):
    return jnp.where(top > NEG, top + jnp.log(total), NEG)


def kept(mask, q, t):
    return jnp.broadcast_to(mask[q * TILES + t : q * TILES + t + 1, :], (BLK, BLK)) > 0


def spread_mask(pos, m00, m01, m10, m11, mask):
    zl, c = pos[2], pos[4]
    left = lax.broadcasted_iota(jnp.int32, (1, BLK), 1) < BLK // 2
    for y in range(Y):
        for dz in range(ZL):
            row = y * 2 + c
            q = y * 2 + jnp.where(dz == 0, zl, 1 - zl)
            for dc, flags in enumerate((m10, m11) if dz else (m00, m01)):
                column = jnp.where(dc == 0, c, 1 - c)
                for x in range(X):
                    lanes = jnp.where(left, flags[row, 2 * x], flags[row, 2 * x + 1])
                    mask[pl.ds(q * TILES + column * X + x, 1), :] = lanes.astype(F32)


def place_images(pos, pieces, k, img):
    source = lax.rem(pos[3] - k + Y, Y)
    for slot in range(2):
        half = jnp.where(slot == 0, pos[2], 1 - pos[2])
        img[pl.ds((source * 2 + half) * BLK, BLK), :] = pieces[slot]
    return source


def score_rows(source, mask, img, cap, s, stats):
    rows = pl.ds(pl.multiple_of(source * 256, 256), 256)
    s[rows, :] = lax.dot_general(
        img[rows, :], cap[...], (((1,), (1,)), ((), ())), preferred_element_type=F32
    )
    for j in range(2):
        q = source * 2 + j
        rows = pl.ds(pl.multiple_of(q * BLK, BLK), BLK)

        def block(t):
            keep = jnp.broadcast_to(mask[pl.ds(q * TILES + t, 1), :], (BLK, BLK)) > 0
            return jnp.where(keep, s[rows, tile(t)] * INVERSE_EPSILON, NEG)

        top = block(0)
        for t in range(1, TILES):
            top = jnp.maximum(top, block(t))
        top_col = jnp.max(top, axis=1, keepdims=True)
        total = jnp.zeros((BLK, BLK), F32)
        for t in range(TILES):
            total = total + jnp.exp(block(t) - top_col)
        value = log_sum(jnp.max(top.T, axis=0, keepdims=True), jnp.sum(total.T, axis=0, keepdims=True))
        for peer in range(N_TXT):
            stats[peer, 0, pl.ds(q, 1), :] = value


def scores_kernel(
    pos, m00, m01, m10, m11, i0, i1, i3, c0, c1, c2, c3, d0, d1, d2, d3, img, cap, s, stats, mask
):
    x, zh, c = pos[0], pos[1], pos[4]
    spread_mask(pos, m00, m01, m10, m11, mask)
    for k, (own, other) in enumerate(((c0, d0), (c1, d1), (c2, d2), (c3, d3))):
        source = lax.rem(x - k + X, X)
        for j in range(ZH):
            place = lax.rem(zh - j + ZH, ZH) * 32
            cap[pl.ds((c * X + source) * BLK + place, 32), :] = own[j]
            cap[pl.ds(((1 - c) * X + source) * BLK + place, 32), :] = other[j]
    for k, pieces in ((0, i0), (1, i1), (3, i3)):
        source = place_images(pos, pieces, k, img)
        score_rows(source, mask, img, cap, s, stats)


def last_scores_kernel(pos, i2, cap, mask, img_in, s_in, stats_in, img, s, stats):
    source = place_images(pos, i2, 2, img)
    score_rows(source, mask, img, cap, s, stats)


def joined(stats):
    top = jnp.max(stats[:, 0], axis=0)
    return top, jnp.sum(jnp.exp(stats[:, 0] - top[None]), axis=0)


def kernel_matrix(mask, row_stats, s, e, stats, top_out, u_vec, u_rows):
    top, total = joined(row_stats)
    u_vec[...] = -(top + jnp.log(total))
    spread_rows(u_vec, u_rows)
    @pl.loop(0, TILES)
    def _(t):
        columns = pl.ds(pl.multiple_of(t * BLK, BLK), BLK)

        def masked(q):
            w = s[tile(q), columns] * INVERSE_EPSILON + u_rows[tile(q), :]
            keep = jnp.broadcast_to(mask[pl.ds(q * TILES + t, 1), :], (BLK, BLK)) > 0
            return keep, jnp.where(keep, w, NEG)

        top = masked(0)[1]
        for q in range(1, TILES):
            top = jnp.maximum(top, masked(q)[1])
        top_row = jnp.max(top, axis=0, keepdims=True)
        total = jnp.zeros((BLK, BLK), F32)
        for q in range(TILES):
            keep, w = masked(q)
            value = jnp.where(keep, jnp.exp(w - top_row), 0.0)
            e[tile(q), columns] = value
            total = total + value
        top_out[pl.ds(t, 1), :] = top_row
        value = log_sum(top_row, jnp.sum(total, axis=0, keepdims=True))
        for peer in range(N_IMG):
            stats[peer, 0, pl.ds(t, 1), :] = value


def first_row_pass(col_stats, own_top, e, x, f, fb0):
    top, total = joined(col_stats)
    mine = own_top[...]
    f[...] = RATIO * jnp.exp(mine - top) / total
    fb0[...] = jnp.exp(mine)
    row_totals(x, 0, lambda q, t: e[tile(q), tile(t)] * f[t : t + 1, :])


def col_pass(x_all, f, e, y, a, rows):
    a[...] = 1.0 / jnp.sum(x_all[:, 0], axis=0)
    spread_rows(a, rows)
    col_totals(y, 0, lambda q, t: e[tile(q), tile(t)] * rows[tile(q), :], f[...])


def row_pass(y_all, f, e, x, b, fb):
    b[...] = RATIO / jnp.sum(y_all[:, 0], axis=0)
    fb[...] = f[...] * b[...]
    row_totals(x, 0, lambda q, t: e[tile(q), tile(t)] * fb[t : t + 1, :])


def last_col_pass(x_all, f, e, s, y, a, rows):
    a[...] = 1.0 / jnp.sum(x_all[:, 0], axis=0)
    spread_rows(a, rows)
    scale = f[...]
    for t in range(TILES):
        total = jnp.zeros((BLK, BLK), F32)
        scored = jnp.zeros((BLK, BLK), F32)
        for q in range(TILES):
            value = e[tile(q), tile(t)] * rows[tile(q), :]
            total = total + value
            scored = scored + value * s[tile(q), tile(t)]
        put_all(y, 0, t, jnp.sum(total, axis=0, keepdims=True) * scale[t : t + 1, :])
        put_all(y, 1, t, jnp.sum(scored, axis=0, keepdims=True) * scale[t : t + 1, :])


def gu3_pass(y_all, f, a3, e, s, x, b3, gv3, c0, c1):
    b3[...] = RATIO / jnp.sum(y_all[:, 0], axis=0)
    gv3[...] = -b3[...] * jnp.sum(y_all[:, 1], axis=0)
    c1[...] = f[...] * b3[...]
    c0[...] = c1[...] * gv3[...] * (1.0 / RATIO)
    row_totals(
        x, 0, lambda q, t: e[tile(q), tile(t)] * (s[tile(q), tile(t)] * c1[t : t + 1, :] + c0[t : t + 1, :])
    )


def gv_pass(x_all, a, f, b, e, y, rows, agu, *, scale):
    gu = -scale * a[...] * jnp.sum(x_all[:, 0], axis=0)
    agu[...] = a[...] * gu
    spread_rows(agu, rows)
    col_totals(y, 0, lambda q, t: e[tile(q), tile(t)] * rows[tile(q), :], -(f[...] * b[...]))


def gu_pass(y_all, f, b, e, x, bgv, c):
    bgv[...] = b[...] * jnp.sum(y_all[:, 0], axis=0)
    c[...] = f[...] * bgv[...]
    row_totals(x, 0, lambda q, t: e[tile(q), tile(t)] * c[t : t + 1, :])


def captions_kernel(
    pos, x_all, r_a2, r_a3, r_gu2, r_gu3, f, fb0, b2, b3, gv3, bgv2, gv1, e, s, img,
    gs, mine, other, vec, r_gu1, k,
):
    vec[...] = (-INVERSE_EPSILON / RATIO) * jnp.sum(x_all[:, 0], axis=0)
    spread_rows(vec, r_gu1)
    scale = f[...]
    k[0] = -INVERSE_EPSILON * (scale * b3[...])
    k[1] = -(scale * b3[...]) * (1.0 + gv3[...])
    k[2] = -scale * bgv2[...]
    k[3] = -scale * gv1[...]
    k[4] = -INVERSE_EPSILON * (scale * b2[...])
    k[5] = -INVERSE_EPSILON * scale
    k[6] = -fb0[...]

    @pl.loop(0, TILES)
    def _(t):
        columns = pl.ds(pl.multiple_of(t * BLK, BLK), BLK)
        k_s, k_a3, k_a2, k_1, k_gu3, k_gu2, k_gu1 = (k[i, pl.ds(t, 1), :] for i in range(7))
        for q in range(TILES):
            rows = tile(q)
            value = (
                r_a3[rows, :] * (k_a3 + k_s * s[rows, columns])
                + r_a2[rows, :] * k_a2
                + k_1
                + r_gu3[rows, :] * k_gu3
                + r_gu2[rows, :] * k_gu2
                + r_gu1[rows, :] * k_gu1
            )
            gs[rows, columns] = (value * e[rows, columns]).astype(BF16)

    core = pos[4]
    for out, c in ((other, 1 - core), (mine, core)):
        for half in range(2):
            columns = pl.ds(pl.multiple_of(c * 512 + half * 256, 256), 256)
            out[half * 256 : half * 256 + 256, :] = lax.dot_general(
                gs[:, columns], img[...], (((0,), (0,)), ((), ())), preferred_element_type=F32
            ).astype(out.dtype)


def images_kernel(pos, gs, cap, o0, o1, o3, o2a, o2b):
    y = pos[3]
    for k, out in ((2, None), (1, o1), (3, o3), (0, o0)):
        target = lax.rem(y + k, Y)
        value = jnp.dot(gs[pl.ds(target * 256, 256), :], cap[...], preferred_element_type=F32)
        if k == 2:
            o2a[...] = value[:BLK].astype(BF16)
            o2b[...] = value[BLK:].astype(BF16)
        else:
            out[...] = value.astype(out.dtype)


def split_over_x(pos, mine, received, p0, p1, p2, p3):
    for k, out in enumerate((p0, p1, p2, p3)):
        rows = pl.ds(lax.rem(pos[0] + k, X) * BLK, BLK)
        out[...] = (mine[rows, :] + received[rows, :].astype(F32)).astype(out.dtype)


def split_over_zh(pos, own, r1, r2, r3, p0, p1, p2, p3):
    for k, out in enumerate((p0, p1, p2, p3)):
        rows = pl.ds(lax.rem(pos[1] + k, ZH) * 32, 32)
        total = own[rows, :]
        for r in (r1, r2, r3):
            total = total + r[rows, :].astype(F32)
        out[...] = total.astype(out.dtype)


def add_passing(o1, o3, passing1, passing3, out1, out3):
    out1[:BLK, :] = (o1[:BLK, :].astype(F32) + passing1[...].astype(F32)).astype(BF16)
    out1[BLK:, :] = o1[BLK:, :]
    out3[:BLK, :] = o3[:BLK, :]
    out3[BLK:, :] = (o3[BLK:, :].astype(F32) + passing3[...].astype(F32)).astype(BF16)


def split_over_zl(pos, own, r1, r3, keep, give):
    zl = pos[2]
    for out, half in ((give, 1 - zl), (keep, zl)):
        rows = pl.ds(half * BLK, BLK)
        out[...] = (own[rows, :] + r1[rows, :].astype(F32) + r3[rows, :].astype(F32)).astype(out.dtype)


def shape(dims, dtype=F32):
    return jax.ShapeDtypeStruct(dims, dtype)


VEC = (TILES, BLK)
ROWS = pltpu.VMEM((SIDE, BLK), F32)
SPREAD = jax.ShapeDtypeStruct((SIDE, BLK), F32)


def run(kernel, outs, scratch, smem, *args, limit=6, aliases={}):
    return pl.pallas_call(
        kernel,
        out_shape=outs,
        in_specs=[SMEM] * smem + [VMEM] * (len(args) - smem),
        out_specs=[VMEM] * len(outs),
        scratch_shapes=scratch,
        input_output_aliases=aliases,
        compiler_params=pltpu.CompilerParams(vmem_limit_bytes=limit * MIB),
    )(*args)


def ring(n, k):
    return [(i, (i + k) % n) for i in range(n)]


def over_txt(v):
    return lax.all_to_all(v, ("y", "zl"), 0, 0, tiled=True)


def over_img(v):
    return lax.all_to_all(v, ("x", "zh", "c"), 0, 0, tiled=True)


def over_img2(v):
    both = v + lax.ppermute(v, "c", ring(C, 1))
    return lax.all_to_all(jnp.broadcast_to(both, (N_IMG // C,) + v.shape[1:]), ("x", "zh"), 0, 0, tiled=True)


def on_device(images, captions, tile_mask):
    pos = jnp.stack([lax.axis_index(name) for name in ("x", "zh", "zl", "y", "c")]).astype(jnp.int32)
    swap = ring(2, 1)
    sibling = lax.ppermute(images, "zl", swap)
    z1, z2, z3 = (lax.ppermute(captions, "zh", ring(ZH, k)) for k in (1, 2, 3))
    m10 = lax.ppermute(tile_mask, "zl", swap)
    m00 = jnp.minimum(tile_mask, 1)
    sibling, z1, z2, z3, m00, m10 = lax.optimization_barrier((sibling, z1, z2, z3, m00, m10))
    m01 = lax.ppermute(tile_mask, "c", swap)
    m11 = lax.ppermute(m10, "c", swap)
    cap_z = jnp.stack([captions, z1, z2, z3])
    c1, c2, c3 = (lax.ppermute(cap_z, "x", ring(X, k)) for k in (1, 2, 3))
    sibling, cap_z = lax.optimization_barrier((sibling, cap_z))
    i0 = jnp.stack([images, sibling])
    i1, i3 = (lax.ppermute(i0, "y", ring(Y, k)) for k in (1, 3))
    c1, c3, i1, i3 = lax.optimization_barrier((c1, c3, i1, i3))
    i2 = lax.ppermute(i1, "y", ring(Y, 1))
    caps = [cap_z, c1, c2, c3]
    other_caps = [lax.ppermute(piece, "c", swap) for piece in caps]

    to_txt = shape((N_TXT, 1) + VEC)
    to_img = shape((N_IMG, 1) + VEC)
    square = (SIDE, SIDE)
    img, cap, s, row_stats, mask = run(
        scores_kernel,
        [shape(square, BF16), shape(square, BF16), shape(square), to_txt, shape((TILES * TILES, BLK))],
        [], 5, pos, m00, m01, m10, m11, i0, i1, i3, *caps, *other_caps, limit=10,
    )
    img, s, row_stats = run(
        last_scores_kernel, [shape(square, BF16), shape(square), to_txt],
        [], 1, pos, i2, cap, mask, img, s, row_stats, limit=10, aliases={4: 0, 5: 1, 6: 2},
    )
    e, col_stats, top = run(
        kernel_matrix, [shape(square), to_img, shape(VEC)],
        [pltpu.VMEM(VEC, F32), ROWS], 0, mask, over_txt(row_stats), s,
    )
    x, f, fb0 = run(first_row_pass, [to_txt, shape(VEC), shape(VEC)], [], 0, over_img(col_stats), top, e)
    y, a2, r_a2 = run(col_pass, [to_img, shape(VEC), SPREAD], [], 0, over_txt(x), f, e)
    vec = pltpu.VMEM(VEC, F32)
    x, b2 = run(row_pass, [to_txt, shape(VEC)], [vec], 0, over_img(y), f, e)
    y, a3, r_a3 = run(last_col_pass, [shape((1, 2) + VEC), shape(VEC), SPREAD], [], 0, over_txt(x), f, e, s)
    x, b3, gv3 = run(gu3_pass, [to_txt, shape(VEC), shape(VEC)], [vec, vec], 0, over_img2(y), f, a3, e, s)
    y, r_gu3 = run(functools.partial(gv_pass, scale=1.0), [to_img, SPREAD], [vec], 0, over_txt(x), a3, f, b2, e)
    x, bgv2 = run(gu_pass, [to_txt, shape(VEC)], [vec], 0, over_img(y), f, b2, e)
    one = jnp.ones(VEC, F32)
    y, r_gu2 = run(functools.partial(gv_pass, scale=1.0 / RATIO), [to_img, SPREAD], [vec], 0, over_txt(x), a2, f, one, e)
    x, gv1 = run(gu_pass, [to_txt, shape(VEC)], [vec], 0, over_img(y), f, one, e)
    gs, mine, other = run(
        captions_kernel, [shape(square, BF16), shape((512, SIDE)), shape((512, SIDE), BF16)],
        [vec, ROWS, pltpu.VMEM((7,) + VEC, F32)], 1,
        pos, over_txt(x), r_a2, r_a3, r_gu2, r_gu3, f, fb0, b2, b3, gv3, bgv2, gv1, e, s, img, limit=10,
    )
    other = lax.ppermute(other, "c", swap)
    block, half, part = (2 * BLK, SIDE), (BLK, SIDE), (32, SIDE)
    o0, o1, o3, o2a, o2b = run(
        images_kernel, [shape(block)] + [shape(block, BF16)] * 2 + [shape(half, BF16)] * 2,
        [], 1, pos, gs, cap, limit=10,
    )
    o2a = lax.ppermute(o2a, "y", ring(Y, 1))
    o2b = lax.ppermute(o2b, "y", ring(Y, 3))
    p0, p1, p2, p3 = run(split_over_x, [shape(half)] + [shape(half, BF16)] * 3, [], 1, pos, mine, other)
    p1, p2, p3 = (lax.ppermute(p, "x", ring(X, k)) for k, p in enumerate((p1, p2, p3), 1))
    o2a, o2b, p1, p3 = lax.optimization_barrier((o2a, o2b, p1, p3))
    o1, o3 = run(add_passing, [shape(block, BF16)] * 2, [], 0, o1, o3, o2a, o2b)
    o1 = lax.ppermute(o1, "y", ring(Y, 1))
    o3 = lax.ppermute(o3, "y", ring(Y, 3))
    keep, give = run(split_over_zl, [shape(half), shape(half, BF16)], [], 1, pos, o0, o1, o3)
    images_grad = keep + lax.ppermute(give, "zl", swap).astype(F32)
    q0, q1, q2, q3 = run(split_over_zh, [shape(part)] + [shape(part, BF16)] * 3, [], 1, pos, p0, p1, p2, p3)
    q1, q2, q3 = (lax.ppermute(q, "zh", ring(ZH, k)) for k, q in enumerate((q1, q2, q3), 1))
    captions_grad = q0 + q1.astype(F32) + q2.astype(F32) + q3.astype(F32)
    return (images_grad, captions_grad)


def solution(mesh):
    split = Mesh(mesh.devices.reshape(X, ZH, ZL, Y, C), ("x", "zh", "zl", "y", "c"))
    img, txt = ("x", "zh", "zl"), ("y", "c")
    in_specs = (P(img + txt, None), P(txt + img, None), P(img, txt))
    out_specs = (P(img + txt, None), P(txt + img, None))
    return jax.shard_map(on_device, mesh=split, in_specs=in_specs, out_specs=out_specs, check_vma=False)
```

```python
import functools

import jax
import jax.numpy as jnp
from jax import lax
from jax.experimental import pallas as pl
from jax.experimental.pallas import tpu as pltpu
from jax.sharding import Mesh, PartitionSpec as P

BLK = 128
INVERSE_EPSILON = 4.0
NEG = -1e30
X, ZH, ZL, Y, C = 4, 4, 2, 4, 2
N_IMG, N_TXT = X * ZH * C, Y * ZL
TILES = 8
SIDE = TILES * BLK
F32, BF16 = jnp.float32, jnp.bfloat16
RATIO = 4.0

VMEM = pl.BlockSpec(memory_space=pltpu.VMEM)
SMEM = pl.BlockSpec(memory_space=pltpu.SMEM)
MIB = 1024 * 1024


def tile(index):
    return pl.ds(index * BLK, BLK)


def spread_rows(vec_ref, out_ref):
    for q in range(TILES):
        row = jnp.broadcast_to(vec_ref[q : q + 1, :], (BLK, BLK))
        out_ref[tile(q), :] = row.T


def put_all(out_ref, slot, q, row):
    for peer in range(out_ref.shape[0]):
        out_ref[peer, slot, q : q + 1, :] = row


def row_totals(out_ref, slot, term):
    for q in range(TILES):
        total = term(q, 0)
        for t in range(1, TILES):
            total = total + term(q, t)
        put_all(out_ref, slot, q, jnp.sum(total.T, axis=0, keepdims=True))


def col_totals(out_ref, slot, term, scale):
    for t in range(TILES):
        total = term(0, t)
        for q in range(1, TILES):
            total = total + term(q, t)
        put_all(out_ref, slot, t, jnp.sum(total, axis=0, keepdims=True) * scale[t : t + 1, :])


def log_sum(top, total):
    return jnp.where(top > NEG, top + jnp.log(total), NEG)


def kept(mask, q, t):
    return jnp.broadcast_to(mask[q * TILES + t : q * TILES + t + 1, :], (BLK, BLK)) > 0


def spread_mask(pos, m00, m01, m10, m11, mask):
    zl, c = pos[2], pos[4]
    left = lax.broadcasted_iota(jnp.int32, (1, BLK), 1) < BLK // 2
    for y in range(Y):
        for dz in range(ZL):
            row = y * 2 + c
            q = y * 2 + jnp.where(dz == 0, zl, 1 - zl)
            for dc, flags in enumerate((m10, m11) if dz else (m00, m01)):
                column = jnp.where(dc == 0, c, 1 - c)
                for x in range(X):
                    lanes = jnp.where(left, flags[row, 2 * x], flags[row, 2 * x + 1])
                    mask[pl.ds(q * TILES + column * X + x, 1), :] = lanes.astype(F32)


def place_images(pos, pieces, k, img):
    source = lax.rem(pos[3] - k + Y, Y)
    for slot in range(2):
        half = jnp.where(slot == 0, pos[2], 1 - pos[2])
        img[pl.ds((source * 2 + half) * BLK, BLK), :] = pieces[slot]
    return source


def score_rows(source, mask, img, cap, s, stats):
    rows = pl.ds(pl.multiple_of(source * 256, 256), 256)
    s[rows, :] = lax.dot_general(
        img[rows, :], cap[...], (((1,), (1,)), ((), ())), preferred_element_type=F32
    )
    for j in range(2):
        q = source * 2 + j
        rows = pl.ds(pl.multiple_of(q * BLK, BLK), BLK)

        def block(t):
            keep = jnp.broadcast_to(mask[pl.ds(q * TILES + t, 1), :], (BLK, BLK)) > 0
            return jnp.where(keep, s[rows, tile(t)] * INVERSE_EPSILON, NEG)

        top = block(0)
        for t in range(1, TILES):
            top = jnp.maximum(top, block(t))
        top_col = jnp.max(top, axis=1, keepdims=True)
        total = jnp.zeros((BLK, BLK), F32)
        for t in range(TILES):
            total = total + jnp.exp(block(t) - top_col)
        value = log_sum(jnp.max(top.T, axis=0, keepdims=True), jnp.sum(total.T, axis=0, keepdims=True))
        for peer in range(N_TXT):
            stats[peer, 0, pl.ds(q, 1), :] = value


def scores_kernel(
    pos, m00, m01, m10, m11, i0, i1, i3, c0, c1, c2, c3, d0, d1, d2, d3, img, cap, s, stats, mask
):
    x, zh, c = pos[0], pos[1], pos[4]
    spread_mask(pos, m00, m01, m10, m11, mask)
    for k, (own, other) in enumerate(((c0, d0), (c1, d1), (c2, d2), (c3, d3))):
        source = lax.rem(x - k + X, X)
        for j in range(ZH):
            place = lax.rem(zh - j + ZH, ZH) * 32
            cap[pl.ds((c * X + source) * BLK + place, 32), :] = own[j]
            cap[pl.ds(((1 - c) * X + source) * BLK + place, 32), :] = other[j]
    for k, pieces in ((0, i0), (1, i1), (3, i3)):
        source = place_images(pos, pieces, k, img)
        score_rows(source, mask, img, cap, s, stats)


def last_scores_kernel(pos, i2, cap, mask, img_in, s_in, stats_in, img, s, stats):
    source = place_images(pos, i2, 2, img)
    score_rows(source, mask, img, cap, s, stats)


def joined(stats):
    top = jnp.max(stats[:, 0], axis=0)
    return top, jnp.sum(jnp.exp(stats[:, 0] - top[None]), axis=0)


def kernel_matrix(mask, row_stats, s, e, stats, top_out, u_vec, u_rows):
    top, total = joined(row_stats)
    u_vec[...] = -(top + jnp.log(total))
    spread_rows(u_vec, u_rows)
    @pl.loop(0, TILES, unroll=8)
    def _(t):
        columns = pl.ds(pl.multiple_of(t * BLK, BLK), BLK)

        def masked(q):
            w = s[tile(q), columns] * INVERSE_EPSILON + u_rows[tile(q), :]
            keep = jnp.broadcast_to(mask[pl.ds(q * TILES + t, 1), :], (BLK, BLK)) > 0
            return keep, jnp.where(keep, w, NEG)

        top = masked(0)[1]
        for q in range(1, TILES):
            top = jnp.maximum(top, masked(q)[1])
        top_row = jnp.max(top, axis=0, keepdims=True)
        total = jnp.zeros((BLK, BLK), F32)
        for q in range(TILES):
            keep, w = masked(q)
            value = jnp.where(keep, jnp.exp(w - top_row), 0.0)
            e[tile(q), columns] = value
            total = total + value
        top_out[pl.ds(t, 1), :] = top_row
        value = log_sum(top_row, jnp.sum(total, axis=0, keepdims=True))
        for peer in range(N_IMG):
            stats[peer, 0, pl.ds(t, 1), :] = value


def first_row_pass(col_stats, own_top, e, x, f, fb0):
    top, total = joined(col_stats)
    mine = own_top[...]
    f[...] = RATIO * jnp.exp(mine - top) / total
    fb0[...] = jnp.exp(mine)
    row_totals(x, 0, lambda q, t: e[tile(q), tile(t)] * f[t : t + 1, :])


def col_pass(x_all, f, e, y, a, rows):
    a[...] = 1.0 / jnp.sum(x_all[:, 0], axis=0)
    spread_rows(a, rows)
    col_totals(y, 0, lambda q, t: e[tile(q), tile(t)] * rows[tile(q), :], f[...])


def row_pass(y_all, f, e, x, b, fb):
    b[...] = RATIO / jnp.sum(y_all[:, 0], axis=0)
    fb[...] = f[...] * b[...]
    row_totals(x, 0, lambda q, t: e[tile(q), tile(t)] * fb[t : t + 1, :])


def last_col_pass(x_all, f, e, s, y, a, rows):
    a[...] = 1.0 / jnp.sum(x_all[:, 0], axis=0)
    spread_rows(a, rows)
    scale = f[...]
    for t in range(TILES):
        total = jnp.zeros((BLK, BLK), F32)
        scored = jnp.zeros((BLK, BLK), F32)
        for q in range(TILES):
            value = e[tile(q), tile(t)] * rows[tile(q), :]
            total = total + value
            scored = scored + value * s[tile(q), tile(t)]
        put_all(y, 0, t, jnp.sum(total, axis=0, keepdims=True) * scale[t : t + 1, :])
        put_all(y, 1, t, jnp.sum(scored, axis=0, keepdims=True) * scale[t : t + 1, :])


def gu3_pass(y_all, f, a3, e, s, x, b3, gv3, c0, c1):
    b3[...] = RATIO / jnp.sum(y_all[:, 0], axis=0)
    gv3[...] = -b3[...] * jnp.sum(y_all[:, 1], axis=0)
    c1[...] = f[...] * b3[...]
    c0[...] = c1[...] * gv3[...] * (1.0 / RATIO)
    row_totals(
        x, 0, lambda q, t: e[tile(q), tile(t)] * (s[tile(q), tile(t)] * c1[t : t + 1, :] + c0[t : t + 1, :])
    )


def gv_pass(x_all, a, f, b, e, y, rows, agu, *, scale):
    gu = -scale * a[...] * jnp.sum(x_all[:, 0], axis=0)
    agu[...] = a[...] * gu
    spread_rows(agu, rows)
    col_totals(y, 0, lambda q, t: e[tile(q), tile(t)] * rows[tile(q), :], -(f[...] * b[...]))


def gu_pass(y_all, f, b, e, x, bgv, c):
    bgv[...] = b[...] * jnp.sum(y_all[:, 0], axis=0)
    c[...] = f[...] * bgv[...]
    row_totals(x, 0, lambda q, t: e[tile(q), tile(t)] * c[t : t + 1, :])


def captions_kernel(
    pos, x_all, r_a2, r_a3, r_gu2, r_gu3, f, fb0, b2, b3, gv3, bgv2, gv1, e, s, img,
    gs, mine, other, vec, r_gu1, k,
):
    vec[...] = (-INVERSE_EPSILON / RATIO) * jnp.sum(x_all[:, 0], axis=0)
    spread_rows(vec, r_gu1)
    scale = f[...]
    k[0] = -INVERSE_EPSILON * (scale * b3[...])
    k[1] = -(scale * b3[...]) * (1.0 + gv3[...])
    k[2] = -scale * bgv2[...]
    k[3] = -scale * gv1[...]
    k[4] = -INVERSE_EPSILON * (scale * b2[...])
    k[5] = -INVERSE_EPSILON * scale
    k[6] = -fb0[...]

    @pl.loop(0, TILES, unroll=2)
    def _(t):
        columns = pl.ds(pl.multiple_of(t * BLK, BLK), BLK)
        k_s, k_a3, k_a2, k_1, k_gu3, k_gu2, k_gu1 = (k[i, pl.ds(t, 1), :] for i in range(7))
        for q in range(TILES):
            rows = tile(q)
            value = (
                r_a3[rows, :] * (k_a3 + k_s * s[rows, columns])
                + r_a2[rows, :] * k_a2
                + k_1
                + r_gu3[rows, :] * k_gu3
                + r_gu2[rows, :] * k_gu2
                + r_gu1[rows, :] * k_gu1
            )
            gs[rows, columns] = (value * e[rows, columns]).astype(BF16)

    core = pos[4]
    for out, c in ((other, 1 - core), (mine, core)):
        for half in range(2):
            columns = pl.ds(pl.multiple_of(c * 512 + half * 256, 256), 256)
            out[half * 256 : half * 256 + 256, :] = lax.dot_general(
                gs[:, columns], img[...], (((0,), (0,)), ((), ())), preferred_element_type=F32
            ).astype(out.dtype)


def images_kernel(pos, gs, cap, o0, o1, o3, o2a, o2b):
    y = pos[3]
    for k, out in ((2, None), (1, o1), (3, o3), (0, o0)):
        target = lax.rem(y + k, Y)
        value = jnp.dot(gs[pl.ds(target * 256, 256), :], cap[...], preferred_element_type=F32)
        if k == 2:
            o2a[...] = value[:BLK].astype(BF16)
            o2b[...] = value[BLK:].astype(BF16)
        else:
            out[...] = value.astype(out.dtype)


def split_over_x(pos, mine, received, p0, p1, p2, p3):
    for k, out in enumerate((p0, p1, p2, p3)):
        rows = pl.ds(lax.rem(pos[0] + k, X) * BLK, BLK)
        out[...] = (mine[rows, :] + received[rows, :].astype(F32)).astype(out.dtype)


def split_over_zh(pos, own, r1, r2, r3, p0, p1, p2, p3):
    for k, out in enumerate((p0, p1, p2, p3)):
        rows = pl.ds(lax.rem(pos[1] + k, ZH) * 32, 32)
        total = own[rows, :]
        for r in (r1, r2, r3):
            total = total + r[rows, :].astype(F32)
        out[...] = total.astype(out.dtype)


def add_passing(o1, o3, passing1, passing3, out1, out3):
    out1[:BLK, :] = (o1[:BLK, :].astype(F32) + passing1[...].astype(F32)).astype(BF16)
    out1[BLK:, :] = o1[BLK:, :]
    out3[:BLK, :] = o3[:BLK, :]
    out3[BLK:, :] = (o3[BLK:, :].astype(F32) + passing3[...].astype(F32)).astype(BF16)


def split_over_zl(pos, own, r1, r3, keep, give):
    zl = pos[2]
    for out, half in ((give, 1 - zl), (keep, zl)):
        rows = pl.ds(half * BLK, BLK)
        out[...] = (own[rows, :] + r1[rows, :].astype(F32) + r3[rows, :].astype(F32)).astype(out.dtype)


def shape(dims, dtype=F32):
    return jax.ShapeDtypeStruct(dims, dtype)


VEC = (TILES, BLK)
ROWS = pltpu.VMEM((SIDE, BLK), F32)
SPREAD = jax.ShapeDtypeStruct((SIDE, BLK), F32)


def run(kernel, outs, scratch, smem, *args, limit=6, aliases={}):
    return pl.pallas_call(
        kernel,
        out_shape=outs,
        in_specs=[SMEM] * smem + [VMEM] * (len(args) - smem),
        out_specs=[VMEM] * len(outs),
        scratch_shapes=scratch,
        input_output_aliases=aliases,
        compiler_params=pltpu.CompilerParams(vmem_limit_bytes=limit * MIB),
    )(*args)


def ring(n, k):
    return [(i, (i + k) % n) for i in range(n)]


def over_txt(v):
    return lax.all_to_all(v, ("y", "zl"), 0, 0, tiled=True)


def over_img(v):
    return lax.all_to_all(v, ("x", "zh", "c"), 0, 0, tiled=True)


def over_img2(v):
    both = v + lax.ppermute(v, "c", ring(C, 1))
    return lax.all_to_all(jnp.broadcast_to(both, (N_IMG // C,) + v.shape[1:]), ("x", "zh"), 0, 0, tiled=True)


def on_device(images, captions, tile_mask):
    pos = jnp.stack([lax.axis_index(name) for name in ("x", "zh", "zl", "y", "c")]).astype(jnp.int32)
    swap = ring(2, 1)
    sibling = lax.ppermute(images, "zl", swap)
    z1, z2, z3 = (lax.ppermute(captions, "zh", ring(ZH, k)) for k in (1, 2, 3))
    m10 = lax.ppermute(tile_mask, "zl", swap)
    m00 = jnp.minimum(tile_mask, 1)
    sibling, z1, z2, z3, m00, m10 = lax.optimization_barrier((sibling, z1, z2, z3, m00, m10))
    m01 = lax.ppermute(tile_mask, "c", swap)
    m11 = lax.ppermute(m10, "c", swap)
    cap_z = jnp.stack([captions, z1, z2, z3])
    c1, c2, c3 = (lax.ppermute(cap_z, "x", ring(X, k)) for k in (1, 2, 3))
    sibling, cap_z = lax.optimization_barrier((sibling, cap_z))
    i0 = jnp.stack([images, sibling])
    i1, i3 = (lax.ppermute(i0, "y", ring(Y, k)) for k in (1, 3))
    c1, c3, i1, i3 = lax.optimization_barrier((c1, c3, i1, i3))
    i2 = lax.ppermute(i1, "y", ring(Y, 1))
    caps = [cap_z, c1, c2, c3]
    other_caps = [lax.ppermute(piece, "c", swap) for piece in caps]

    to_txt = shape((N_TXT, 1) + VEC)
    to_img = shape((N_IMG, 1) + VEC)
    square = (SIDE, SIDE)
    img, cap, s, row_stats, mask = run(
        scores_kernel,
        [shape(square, BF16), shape(square, BF16), shape(square), to_txt, shape((TILES * TILES, BLK))],
        [], 5, pos, m00, m01, m10, m11, i0, i1, i3, *caps, *other_caps, limit=10,
    )
    img, s, row_stats = run(
        last_scores_kernel, [shape(square, BF16), shape(square), to_txt],
        [], 1, pos, i2, cap, mask, img, s, row_stats, limit=10, aliases={4: 0, 5: 1, 6: 2},
    )
    e, col_stats, top = run(
        kernel_matrix, [shape(square), to_img, shape(VEC)],
        [pltpu.VMEM(VEC, F32), ROWS], 0, mask, over_txt(row_stats), s,
    )
    x, f, fb0 = run(first_row_pass, [to_txt, shape(VEC), shape(VEC)], [], 0, over_img(col_stats), top, e)
    y, a2, r_a2 = run(col_pass, [to_img, shape(VEC), SPREAD], [], 0, over_txt(x), f, e)
    vec = pltpu.VMEM(VEC, F32)
    x, b2 = run(row_pass, [to_txt, shape(VEC)], [vec], 0, over_img(y), f, e)
    y, a3, r_a3 = run(last_col_pass, [shape((1, 2) + VEC), shape(VEC), SPREAD], [], 0, over_txt(x), f, e, s)
    x, b3, gv3 = run(gu3_pass, [to_txt, shape(VEC), shape(VEC)], [vec, vec], 0, over_img2(y), f, a3, e, s)
    y, r_gu3 = run(functools.partial(gv_pass, scale=1.0), [to_img, SPREAD], [vec], 0, over_txt(x), a3, f, b2, e)
    x, bgv2 = run(gu_pass, [to_txt, shape(VEC)], [vec], 0, over_img(y), f, b2, e)
    one = jnp.ones(VEC, F32)
    y, r_gu2 = run(functools.partial(gv_pass, scale=1.0 / RATIO), [to_img, SPREAD], [vec], 0, over_txt(x), a2, f, one, e)
    x, gv1 = run(gu_pass, [to_txt, shape(VEC)], [vec], 0, over_img(y), f, one, e)
    gs, mine, other = run(
        captions_kernel, [shape(square, BF16), shape((512, SIDE)), shape((512, SIDE), BF16)],
        [vec, ROWS, pltpu.VMEM((7,) + VEC, F32)], 1,
        pos, over_txt(x), r_a2, r_a3, r_gu2, r_gu3, f, fb0, b2, b3, gv3, bgv2, gv1, e, s, img, limit=10,
    )
    other = lax.ppermute(other, "c", swap)
    block, half, part = (2 * BLK, SIDE), (BLK, SIDE), (32, SIDE)
    o0, o1, o3, o2a, o2b = run(
        images_kernel, [shape(block)] + [shape(block, BF16)] * 2 + [shape(half, BF16)] * 2,
        [], 1, pos, gs, cap, limit=10,
    )
    o2a = lax.ppermute(o2a, "y", ring(Y, 1))
    o2b = lax.ppermute(o2b, "y", ring(Y, 3))
    p0, p1, p2, p3 = run(split_over_x, [shape(half)] + [shape(half, BF16)] * 3, [], 1, pos, mine, other)
    p1, p2, p3 = (lax.ppermute(p, "x", ring(X, k)) for k, p in enumerate((p1, p2, p3), 1))
    o2a, o2b, p1, p3 = lax.optimization_barrier((o2a, o2b, p1, p3))
    o1, o3 = run(add_passing, [shape(block, BF16)] * 2, [], 0, o1, o3, o2a, o2b)
    o1 = lax.ppermute(o1, "y", ring(Y, 1))
    o3 = lax.ppermute(o3, "y", ring(Y, 3))
    keep, give = run(split_over_zl, [shape(half), shape(half, BF16)], [], 1, pos, o0, o1, o3)
    images_grad = keep + lax.ppermute(give, "zl", swap).astype(F32)
    q0, q1, q2, q3 = run(split_over_zh, [shape(part)] + [shape(part, BF16)] * 3, [], 1, pos, p0, p1, p2, p3)
    q1, q2, q3 = (lax.ppermute(q, "zh", ring(ZH, k)) for k, q in enumerate((q1, q2, q3), 1))
    captions_grad = q0 + q1.astype(F32) + q2.astype(F32) + q3.astype(F32)
    return (images_grad, captions_grad)


def solution(mesh):
    split = Mesh(mesh.devices.reshape(X, ZH, ZL, Y, C), ("x", "zh", "zl", "y", "c"))
    img, txt = ("x", "zh", "zl"), ("y", "c")
    in_specs = (P(img + txt, None), P(txt + img, None), P(img, txt))
    out_specs = (P(img + txt, None), P(txt + img, None))
    return jax.shard_map(on_device, mesh=split, in_specs=in_specs, out_specs=out_specs, check_vma=False)
```

```python
import functools

import jax
import jax.numpy as jnp
from jax import lax
from jax.experimental import pallas as pl
from jax.experimental.pallas import tpu as pltpu
from jax.sharding import Mesh, PartitionSpec as P

BLK = 128
INVERSE_EPSILON = 4.0
NEG = -1e30
X, ZH, ZL, Y, C = 4, 4, 2, 4, 2
N_IMG, N_TXT = X * ZH * C, Y * ZL
TILES = 8
SIDE = TILES * BLK
F32, BF16 = jnp.float32, jnp.bfloat16
RATIO = 4.0

VMEM = pl.BlockSpec(memory_space=pltpu.VMEM)
SMEM = pl.BlockSpec(memory_space=pltpu.SMEM)
MIB = 1024 * 1024


def tile(index):
    return pl.ds(index * BLK, BLK)


def spread_rows(vec_ref, out_ref):
    for q in range(TILES):
        row = jnp.broadcast_to(vec_ref[q : q + 1, :], (BLK, BLK))
        out_ref[tile(q), :] = row.T


def put_all(out_ref, slot, q, row):
    for peer in range(out_ref.shape[0]):
        out_ref[peer, slot, q : q + 1, :] = row


def row_totals(out_ref, slot, term):
    for q in range(TILES):
        total = term(q, 0)
        for t in range(1, TILES):
            total = total + term(q, t)
        put_all(out_ref, slot, q, jnp.sum(total.T, axis=0, keepdims=True))


def col_totals(out_ref, slot, term, scale):
    for t in range(TILES):
        total = term(0, t)
        for q in range(1, TILES):
            total = total + term(q, t)
        put_all(out_ref, slot, t, jnp.sum(total, axis=0, keepdims=True) * scale[t : t + 1, :])


def log_sum(top, total):
    return jnp.where(top > NEG, top + jnp.log(total), NEG)


def kept(mask, q, t):
    return jnp.broadcast_to(mask[q * TILES + t : q * TILES + t + 1, :], (BLK, BLK)) > 0


def spread_mask(pos, m00, m01, m10, m11, mask):
    zl, c = pos[2], pos[4]
    left = lax.broadcasted_iota(jnp.int32, (1, BLK), 1) < BLK // 2
    for y in range(Y):
        for dz in range(ZL):
            row = y * 2 + c
            q = y * 2 + jnp.where(dz == 0, zl, 1 - zl)
            for dc, flags in enumerate((m10, m11) if dz else (m00, m01)):
                column = jnp.where(dc == 0, c, 1 - c)
                for x in range(X):
                    lanes = jnp.where(left, flags[row, 2 * x], flags[row, 2 * x + 1])
                    mask[pl.ds(q * TILES + column * X + x, 1), :] = lanes.astype(F32)


def place_images(pos, pieces, k, img):
    source = lax.rem(pos[3] - k + Y, Y)
    for slot in range(2):
        half = jnp.where(slot == 0, pos[2], 1 - pos[2])
        img[pl.ds((source * 2 + half) * BLK, BLK), :] = pieces[slot]
    return source


def score_rows(source, mask, img, cap, s, stats):
    rows = pl.ds(pl.multiple_of(source * 256, 256), 256)
    s[rows, :] = lax.dot_general(
        img[rows, :], cap[...], (((1,), (1,)), ((), ())), preferred_element_type=F32
    )
    for j in range(2):
        q = source * 2 + j
        rows = pl.ds(pl.multiple_of(q * BLK, BLK), BLK)

        def block(t):
            keep = jnp.broadcast_to(mask[pl.ds(q * TILES + t, 1), :], (BLK, BLK)) > 0
            return jnp.where(keep, s[rows, tile(t)] * INVERSE_EPSILON, NEG)

        top = block(0)
        for t in range(1, TILES):
            top = jnp.maximum(top, block(t))
        top_col = jnp.max(top, axis=1, keepdims=True)
        total = jnp.zeros((BLK, BLK), F32)
        for t in range(TILES):
            total = total + jnp.exp(block(t) - top_col)
        value = log_sum(jnp.max(top.T, axis=0, keepdims=True), jnp.sum(total.T, axis=0, keepdims=True))
        for peer in range(N_TXT):
            stats[peer, 0, pl.ds(q, 1), :] = value


def scores_kernel(
    pos, m00, m01, m10, m11, i0, i1, i3, c0, c1, c2, c3, d0, d1, d2, d3, img, cap, s, stats, mask
):
    x, zh, c = pos[0], pos[1], pos[4]
    spread_mask(pos, m00, m01, m10, m11, mask)
    for k, (own, other) in enumerate(((c0, d0), (c1, d1), (c2, d2), (c3, d3))):
        source = lax.rem(x - k + X, X)
        for j in range(ZH):
            place = lax.rem(zh - j + ZH, ZH) * 32
            cap[pl.ds((c * X + source) * BLK + place, 32), :] = own[j]
            cap[pl.ds(((1 - c) * X + source) * BLK + place, 32), :] = other[j]
    for k, pieces in ((0, i0), (1, i1), (3, i3)):
        place_images(pos, pieces, k, img)

    @pl.loop(0, 3)
    def _(j):
        k = j + j // 2
        score_rows(lax.rem(pos[3] - k + Y, Y), mask, img, cap, s, stats)


def last_scores_kernel(pos, i2, cap, mask, img_in, s_in, stats_in, img, s, stats):
    source = place_images(pos, i2, 2, img)
    score_rows(source, mask, img, cap, s, stats)


def joined(stats):
    top = jnp.max(stats[:, 0], axis=0)
    return top, jnp.sum(jnp.exp(stats[:, 0] - top[None]), axis=0)


def kernel_matrix(mask, row_stats, s, e, stats, top_out, u_vec, u_rows):
    top, total = joined(row_stats)
    u_vec[...] = -(top + jnp.log(total))
    spread_rows(u_vec, u_rows)
    @pl.loop(0, TILES, unroll=8)
    def _(t):
        columns = pl.ds(pl.multiple_of(t * BLK, BLK), BLK)

        def masked(q):
            w = s[tile(q), columns] * INVERSE_EPSILON + u_rows[tile(q), :]
            keep = jnp.broadcast_to(mask[pl.ds(q * TILES + t, 1), :], (BLK, BLK)) > 0
            return keep, jnp.where(keep, w, NEG)

        top = masked(0)[1]
        for q in range(1, TILES):
            top = jnp.maximum(top, masked(q)[1])
        top_row = jnp.max(top, axis=0, keepdims=True)
        total = jnp.zeros((BLK, BLK), F32)
        for q in range(TILES):
            keep, w = masked(q)
            value = jnp.where(keep, jnp.exp(w - top_row), 0.0)
            e[tile(q), columns] = value
            total = total + value
        top_out[pl.ds(t, 1), :] = top_row
        value = log_sum(top_row, jnp.sum(total, axis=0, keepdims=True))
        for peer in range(N_IMG):
            stats[peer, 0, pl.ds(t, 1), :] = value


def first_row_pass(col_stats, own_top, e, x, f, fb0):
    top, total = joined(col_stats)
    mine = own_top[...]
    f[...] = RATIO * jnp.exp(mine - top) / total
    fb0[...] = jnp.exp(mine)
    row_totals(x, 0, lambda q, t: e[tile(q), tile(t)] * f[t : t + 1, :])


def col_pass(x_all, f, e, y, a, rows):
    a[...] = 1.0 / jnp.sum(x_all[:, 0], axis=0)
    spread_rows(a, rows)
    col_totals(y, 0, lambda q, t: e[tile(q), tile(t)] * rows[tile(q), :], f[...])


def row_pass(y_all, f, e, x, b, fb):
    b[...] = RATIO / jnp.sum(y_all[:, 0], axis=0)
    fb[...] = f[...] * b[...]
    row_totals(x, 0, lambda q, t: e[tile(q), tile(t)] * fb[t : t + 1, :])


def last_col_pass(x_all, f, e, s, y, a, rows):
    a[...] = 1.0 / jnp.sum(x_all[:, 0], axis=0)
    spread_rows(a, rows)
    scale = f[...]
    for t in range(TILES):
        total = jnp.zeros((BLK, BLK), F32)
        scored = jnp.zeros((BLK, BLK), F32)
        for q in range(TILES):
            value = e[tile(q), tile(t)] * rows[tile(q), :]
            total = total + value
            scored = scored + value * s[tile(q), tile(t)]
        put_all(y, 0, t, jnp.sum(total, axis=0, keepdims=True) * scale[t : t + 1, :])
        put_all(y, 1, t, jnp.sum(scored, axis=0, keepdims=True) * scale[t : t + 1, :])


def gu3_pass(y_all, f, a3, e, s, x, b3, gv3, c0, c1):
    b3[...] = RATIO / jnp.sum(y_all[:, 0], axis=0)
    gv3[...] = -b3[...] * jnp.sum(y_all[:, 1], axis=0)
    c1[...] = f[...] * b3[...]
    c0[...] = c1[...] * gv3[...] * (1.0 / RATIO)
    row_totals(
        x, 0, lambda q, t: e[tile(q), tile(t)] * (s[tile(q), tile(t)] * c1[t : t + 1, :] + c0[t : t + 1, :])
    )


def gv_pass(x_all, a, f, b, e, y, rows, agu, *, scale):
    gu = -scale * a[...] * jnp.sum(x_all[:, 0], axis=0)
    agu[...] = a[...] * gu
    spread_rows(agu, rows)
    col_totals(y, 0, lambda q, t: e[tile(q), tile(t)] * rows[tile(q), :], -(f[...] * b[...]))


def gu_pass(y_all, f, b, e, x, bgv, c):
    bgv[...] = b[...] * jnp.sum(y_all[:, 0], axis=0)
    c[...] = f[...] * bgv[...]
    row_totals(x, 0, lambda q, t: e[tile(q), tile(t)] * c[t : t + 1, :])


def captions_kernel(
    pos, x_all, r_a2, r_a3, r_gu2, r_gu3, f, fb0, b2, b3, gv3, bgv2, gv1, e, s, img,
    gs, mine, other, vec, r_gu1, k,
):
    vec[...] = (-INVERSE_EPSILON / RATIO) * jnp.sum(x_all[:, 0], axis=0)
    spread_rows(vec, r_gu1)
    scale = f[...]
    k[0] = -INVERSE_EPSILON * (scale * b3[...])
    k[1] = -(scale * b3[...]) * (1.0 + gv3[...])
    k[2] = -scale * bgv2[...]
    k[3] = -scale * gv1[...]
    k[4] = -INVERSE_EPSILON * (scale * b2[...])
    k[5] = -INVERSE_EPSILON * scale
    k[6] = -fb0[...]

    @pl.loop(0, TILES)
    def _(t):
        columns = pl.ds(pl.multiple_of(t * BLK, BLK), BLK)
        k_s, k_a3, k_a2, k_1, k_gu3, k_gu2, k_gu1 = (k[i, pl.ds(t, 1), :] for i in range(7))
        for q in range(TILES):
            rows = tile(q)
            value = (
                r_a3[rows, :] * (k_a3 + k_s * s[rows, columns])
                + r_a2[rows, :] * k_a2
                + k_1
                + r_gu3[rows, :] * k_gu3
                + r_gu2[rows, :] * k_gu2
                + r_gu1[rows, :] * k_gu1
            )
            gs[rows, columns] = (value * e[rows, columns]).astype(BF16)

    core = pos[4]
    for out, c in ((other, 1 - core), (mine, core)):
        for half in range(2):
            columns = pl.ds(pl.multiple_of(c * 512 + half * 256, 256), 256)
            out[half * 256 : half * 256 + 256, :] = lax.dot_general(
                gs[:, columns], img[...], (((0,), (0,)), ((), ())), preferred_element_type=F32
            ).astype(out.dtype)


def image_rows(pos, gs, cap, k):
    target = lax.rem(pos[3] + k, Y)
    return jnp.dot(gs[pl.ds(target * 256, 256), :], cap[...], preferred_element_type=F32)


def passing_images_kernel(pos, gs, cap, o2a, o2b):
    value = image_rows(pos, gs, cap, 2)
    o2a[...] = value[:BLK].astype(BF16)
    o2b[...] = value[BLK:].astype(BF16)


def images_kernel(pos, gs, cap, o0, o1, o3):
    for k, out in ((1, o1), (3, o3), (0, o0)):
        out[...] = image_rows(pos, gs, cap, k).astype(out.dtype)


def split_over_x(pos, mine, received, p0, p1, p2, p3):
    for k, out in enumerate((p0, p1, p2, p3)):
        rows = pl.ds(lax.rem(pos[0] + k, X) * BLK, BLK)
        out[...] = (mine[rows, :] + received[rows, :].astype(F32)).astype(out.dtype)


def split_over_zh(pos, own, r1, r2, r3, p0, p1, p2, p3):
    for k, out in enumerate((p0, p1, p2, p3)):
        rows = pl.ds(lax.rem(pos[1] + k, ZH) * 32, 32)
        total = own[rows, :]
        for r in (r1, r2, r3):
            total = total + r[rows, :].astype(F32)
        out[...] = total.astype(out.dtype)


def add_passing(o1, o3, passing1, passing3, out1, out3):
    out1[:BLK, :] = (o1[:BLK, :].astype(F32) + passing1[...].astype(F32)).astype(BF16)
    out1[BLK:, :] = o1[BLK:, :]
    out3[:BLK, :] = o3[:BLK, :]
    out3[BLK:, :] = (o3[BLK:, :].astype(F32) + passing3[...].astype(F32)).astype(BF16)


def split_over_zl(pos, own, r1, r3, keep, give):
    zl = pos[2]
    for out, half in ((give, 1 - zl), (keep, zl)):
        rows = pl.ds(half * BLK, BLK)
        out[...] = (own[rows, :] + r1[rows, :].astype(F32) + r3[rows, :].astype(F32)).astype(out.dtype)


def shape(dims, dtype=F32):
    return jax.ShapeDtypeStruct(dims, dtype)


VEC = (TILES, BLK)
ROWS = pltpu.VMEM((SIDE, BLK), F32)
SPREAD = jax.ShapeDtypeStruct((SIDE, BLK), F32)


def run(kernel, outs, scratch, smem, *args, limit=6, aliases={}):
    return pl.pallas_call(
        kernel,
        out_shape=outs,
        in_specs=[SMEM] * smem + [VMEM] * (len(args) - smem),
        out_specs=[VMEM] * len(outs),
        scratch_shapes=scratch,
        input_output_aliases=aliases,
        compiler_params=pltpu.CompilerParams(vmem_limit_bytes=limit * MIB),
    )(*args)


def ring(n, k):
    return [(i, (i + k) % n) for i in range(n)]


def over_txt(v):
    return lax.all_to_all(v, ("y", "zl"), 0, 0, tiled=True)


def over_img(v):
    return lax.all_to_all(v, ("x", "zh", "c"), 0, 0, tiled=True)


def over_img2(v):
    both = v + lax.ppermute(v, "c", ring(C, 1))
    return lax.all_to_all(jnp.broadcast_to(both, (N_IMG // C,) + v.shape[1:]), ("x", "zh"), 0, 0, tiled=True)


def on_device(images, captions, tile_mask):
    pos = jnp.stack([lax.axis_index(name) for name in ("x", "zh", "zl", "y", "c")]).astype(jnp.int32)
    swap = ring(2, 1)
    sibling = lax.ppermute(images, "zl", swap)
    z1, z2, z3 = (lax.ppermute(captions, "zh", ring(ZH, k)) for k in (1, 2, 3))
    m10 = lax.ppermute(tile_mask, "zl", swap)
    m00 = jnp.minimum(tile_mask, 1)
    sibling, z1, z2, z3, m00, m10 = lax.optimization_barrier((sibling, z1, z2, z3, m00, m10))
    m01 = lax.ppermute(tile_mask, "c", swap)
    m11 = lax.ppermute(m10, "c", swap)
    cap_z = jnp.stack([captions, z1, z2, z3])
    c1, c2, c3 = (lax.ppermute(cap_z, "x", ring(X, k)) for k in (1, 2, 3))
    sibling, cap_z = lax.optimization_barrier((sibling, cap_z))
    i0 = jnp.stack([images, sibling])
    i1, i3 = (lax.ppermute(i0, "y", ring(Y, k)) for k in (1, 3))
    c1, c3, i1, i3 = lax.optimization_barrier((c1, c3, i1, i3))
    i2 = lax.ppermute(i1, "y", ring(Y, 1))
    caps = [cap_z, c1, c2, c3]
    other_caps = [lax.ppermute(piece, "c", swap) for piece in caps]

    to_txt = shape((N_TXT, 1) + VEC)
    to_img = shape((N_IMG, 1) + VEC)
    square = (SIDE, SIDE)
    img, cap, s, row_stats, mask = run(
        scores_kernel,
        [shape(square, BF16), shape(square, BF16), shape(square), to_txt, shape((TILES * TILES, BLK))],
        [], 5, pos, m00, m01, m10, m11, i0, i1, i3, *caps, *other_caps, limit=10,
    )
    img, s, row_stats = run(
        last_scores_kernel, [shape(square, BF16), shape(square), to_txt],
        [], 1, pos, i2, cap, mask, img, s, row_stats, limit=10, aliases={4: 0, 5: 1, 6: 2},
    )
    e, col_stats, top = run(
        kernel_matrix, [shape(square), to_img, shape(VEC)],
        [pltpu.VMEM(VEC, F32), ROWS], 0, mask, over_txt(row_stats), s,
    )
    x, f, fb0 = run(first_row_pass, [to_txt, shape(VEC), shape(VEC)], [], 0, over_img(col_stats), top, e)
    y, a2, r_a2 = run(col_pass, [to_img, shape(VEC), SPREAD], [], 0, over_txt(x), f, e)
    vec = pltpu.VMEM(VEC, F32)
    x, b2 = run(row_pass, [to_txt, shape(VEC)], [vec], 0, over_img(y), f, e)
    y, a3, r_a3 = run(last_col_pass, [shape((1, 2) + VEC), shape(VEC), SPREAD], [], 0, over_txt(x), f, e, s)
    x, b3, gv3 = run(gu3_pass, [to_txt, shape(VEC), shape(VEC)], [vec, vec], 0, over_img2(y), f, a3, e, s)
    y, r_gu3 = run(functools.partial(gv_pass, scale=1.0), [to_img, SPREAD], [vec], 0, over_txt(x), a3, f, b2, e)
    x, bgv2 = run(gu_pass, [to_txt, shape(VEC)], [vec], 0, over_img(y), f, b2, e)
    one = jnp.ones(VEC, F32)
    y, r_gu2 = run(functools.partial(gv_pass, scale=1.0 / RATIO), [to_img, SPREAD], [vec], 0, over_txt(x), a2, f, one, e)
    x, gv1 = run(gu_pass, [to_txt, shape(VEC)], [vec], 0, over_img(y), f, one, e)
    gs, mine, other = run(
        captions_kernel, [shape(square, BF16), shape((512, SIDE)), shape((512, SIDE), BF16)],
        [vec, ROWS, pltpu.VMEM((7,) + VEC, F32)], 1,
        pos, over_txt(x), r_a2, r_a3, r_gu2, r_gu3, f, fb0, b2, b3, gv3, bgv2, gv1, e, s, img, limit=10,
    )
    other = lax.ppermute(other, "c", swap)
    block, half, part = (2 * BLK, SIDE), (BLK, SIDE), (32, SIDE)
    o2a, o2b = run(passing_images_kernel, [shape(half, BF16)] * 2, [], 1, pos, gs, cap, limit=10)
    o0, o1, o3 = run(
        images_kernel, [shape(block)] + [shape(block, BF16)] * 2, [], 1, pos, gs, cap, limit=10,
    )
    o2a = lax.ppermute(o2a, "y", ring(Y, 1))
    o2b = lax.ppermute(o2b, "y", ring(Y, 3))
    p0, p1, p2, p3 = run(split_over_x, [shape(half)] + [shape(half, BF16)] * 3, [], 1, pos, mine, other)
    p1, p2, p3 = (lax.ppermute(p, "x", ring(X, k)) for k, p in enumerate((p1, p2, p3), 1))
    o2a, o2b, p1, p3 = lax.optimization_barrier((o2a, o2b, p1, p3))
    o1, o3 = run(add_passing, [shape(block, BF16)] * 2, [], 0, o1, o3, o2a, o2b)
    o1 = lax.ppermute(o1, "y", ring(Y, 1))
    o3 = lax.ppermute(o3, "y", ring(Y, 3))
    keep, give = run(split_over_zl, [shape(half), shape(half, BF16)], [], 1, pos, o0, o1, o3)
    images_grad = keep + lax.ppermute(give, "zl", swap).astype(F32)
    q0, q1, q2, q3 = run(split_over_zh, [shape(part)] + [shape(part, BF16)] * 3, [], 1, pos, p0, p1, p2, p3)
    q1, q2, q3 = (lax.ppermute(q, "zh", ring(ZH, k)) for k, q in enumerate((q1, q2, q3), 1))
    captions_grad = q0 + q1.astype(F32) + q2.astype(F32) + q3.astype(F32)
    return (images_grad, captions_grad)


def solution(mesh):
    split = Mesh(mesh.devices.reshape(X, ZH, ZL, Y, C), ("x", "zh", "zl", "y", "c"))
    img, txt = ("x", "zh", "zl"), ("y", "c")
    in_specs = (P(img + txt, None), P(txt + img, None), P(img, txt))
    out_specs = (P(img + txt, None), P(txt + img, None))
    return jax.shard_map(on_device, mesh=split, in_specs=in_specs, out_specs=out_specs, check_vma=False)
```

```python
import functools

import jax
import jax.numpy as jnp
from jax import lax
from jax.experimental import pallas as pl
from jax.experimental.pallas import tpu as pltpu
from jax.sharding import Mesh, PartitionSpec as P

BLK = 128
INVERSE_EPSILON = 4.0
NEG = -1e30
X, ZH, ZL, Y, C = 4, 4, 2, 4, 2
N_IMG, N_TXT = X * ZH * C, Y * ZL
TILES = 8
SIDE = TILES * BLK
F32, BF16 = jnp.float32, jnp.bfloat16
RATIO = 4.0

VMEM = pl.BlockSpec(memory_space=pltpu.VMEM)
SMEM = pl.BlockSpec(memory_space=pltpu.SMEM)
MIB = 1024 * 1024


def tile(index):
    return pl.ds(index * BLK, BLK)


def spread_rows(vec_ref, out_ref):
    for q in range(TILES):
        row = jnp.broadcast_to(vec_ref[q : q + 1, :], (BLK, BLK))
        out_ref[tile(q), :] = row.T


def put_all(out_ref, slot, q, row):
    for peer in range(out_ref.shape[0]):
        out_ref[peer, slot, q : q + 1, :] = row


def row_totals(out_ref, slot, term):
    for q in range(TILES):
        total = term(q, 0)
        for t in range(1, TILES):
            total = total + term(q, t)
        put_all(out_ref, slot, q, jnp.sum(total.T, axis=0, keepdims=True))


def col_totals(out_ref, slot, term, scale):
    for t in range(TILES):
        total = term(0, t)
        for q in range(1, TILES):
            total = total + term(q, t)
        put_all(out_ref, slot, t, jnp.sum(total, axis=0, keepdims=True) * scale[t : t + 1, :])


def log_sum(top, total):
    return jnp.where(top > NEG, top + jnp.log(total), NEG)


def kept(mask, q, t):
    return jnp.broadcast_to(mask[q * TILES + t : q * TILES + t + 1, :], (BLK, BLK)) > 0


def spread_mask(pos, m00, m01, m10, m11, mask):
    zl, c = pos[2], pos[4]
    left = lax.broadcasted_iota(jnp.int32, (1, BLK), 1) < BLK // 2
    for y in range(Y):
        for dz in range(ZL):
            row = y * 2 + c
            q = y * 2 + jnp.where(dz == 0, zl, 1 - zl)
            for dc, flags in enumerate((m10, m11) if dz else (m00, m01)):
                column = jnp.where(dc == 0, c, 1 - c)
                for x in range(X):
                    lanes = jnp.where(left, flags[row, 2 * x], flags[row, 2 * x + 1])
                    mask[pl.ds(q * TILES + column * X + x, 1), :] = lanes.astype(F32)


def place_images(pos, pieces, k, img):
    source = lax.rem(pos[3] - k + Y, Y)
    for slot in range(2):
        half = jnp.where(slot == 0, pos[2], 1 - pos[2])
        img[pl.ds((source * 2 + half) * BLK, BLK), :] = pieces[slot]
    return source


def score_rows(source, mask, img, cap, s, stats):
    rows = pl.ds(pl.multiple_of(source * 256, 256), 256)
    s[rows, :] = lax.dot_general(
        img[rows, :], cap[...], (((1,), (1,)), ((), ())), preferred_element_type=F32
    )
    for j in range(2):
        q = source * 2 + j
        rows = pl.ds(pl.multiple_of(q * BLK, BLK), BLK)

        def block(t):
            keep = jnp.broadcast_to(mask[pl.ds(q * TILES + t, 1), :], (BLK, BLK)) > 0
            return jnp.where(keep, s[rows, tile(t)] * INVERSE_EPSILON, NEG)

        top = block(0)
        for t in range(1, TILES):
            top = jnp.maximum(top, block(t))
        top_col = jnp.max(top, axis=1, keepdims=True)
        total = jnp.zeros((BLK, BLK), F32)
        for t in range(TILES):
            total = total + jnp.exp(block(t) - top_col)
        value = log_sum(jnp.max(top.T, axis=0, keepdims=True), jnp.sum(total.T, axis=0, keepdims=True))
        for peer in range(N_TXT):
            stats[peer, 0, pl.ds(q, 1), :] = value


def scores_kernel(
    pos, m00, m01, m10, m11, i0, i1, i3, c0, c1, c2, c3, d0, d1, d2, d3, img, cap, s, stats, mask
):
    x, zh, c = pos[0], pos[1], pos[4]
    spread_mask(pos, m00, m01, m10, m11, mask)
    for k, (own, other) in enumerate(((c0, d0), (c1, d1), (c2, d2), (c3, d3))):
        source = lax.rem(x - k + X, X)
        for j in range(ZH):
            place = lax.rem(zh - j + ZH, ZH) * 32
            cap[pl.ds((c * X + source) * BLK + place, 32), :] = own[j]
            cap[pl.ds(((1 - c) * X + source) * BLK + place, 32), :] = other[j]
    for k, pieces in ((0, i0), (1, i1), (3, i3)):
        place_images(pos, pieces, k, img)

    @pl.loop(0, 3)
    def _(j):
        k = j + j // 2
        score_rows(lax.rem(pos[3] - k + Y, Y), mask, img, cap, s, stats)


def last_scores_kernel(pos, i2, cap, mask, img_in, s_in, stats_in, img, s, stats):
    source = place_images(pos, i2, 2, img)
    score_rows(source, mask, img, cap, s, stats)


def joined(stats):
    top = jnp.max(stats[:, 0], axis=0)
    return top, jnp.sum(jnp.exp(stats[:, 0] - top[None]), axis=0)


def kernel_matrix(mask, row_stats, s, e, stats, top_out, u_vec, u_rows):
    top, total = joined(row_stats)
    u_vec[...] = -(top + jnp.log(total))
    spread_rows(u_vec, u_rows)
    @pl.loop(0, TILES, unroll=8)
    def _(t):
        columns = pl.ds(pl.multiple_of(t * BLK, BLK), BLK)

        def masked(q):
            w = s[tile(q), columns] * INVERSE_EPSILON + u_rows[tile(q), :]
            keep = jnp.broadcast_to(mask[pl.ds(q * TILES + t, 1), :], (BLK, BLK)) > 0
            return keep, jnp.where(keep, w, NEG)

        top = masked(0)[1]
        for q in range(1, TILES):
            top = jnp.maximum(top, masked(q)[1])
        top_row = jnp.max(top, axis=0, keepdims=True)
        total = jnp.zeros((BLK, BLK), F32)
        for q in range(TILES):
            keep, w = masked(q)
            value = jnp.where(keep, jnp.exp(w - top_row), 0.0)
            e[tile(q), columns] = value
            total = total + value
        top_out[pl.ds(t, 1), :] = top_row
        value = log_sum(top_row, jnp.sum(total, axis=0, keepdims=True))
        for peer in range(N_IMG):
            stats[peer, 0, pl.ds(t, 1), :] = value


def first_row_pass(col_stats, own_top, e, x, f, fb0):
    top, total = joined(col_stats)
    mine = own_top[...]
    f[...] = RATIO * jnp.exp(mine - top) / total
    fb0[...] = jnp.exp(mine)
    row_totals(x, 0, lambda q, t: e[tile(q), tile(t)] * f[t : t + 1, :])


def col_pass(x_all, f, e, y, a, rows):
    a[...] = 1.0 / jnp.sum(x_all[:, 0], axis=0)
    spread_rows(a, rows)
    col_totals(y, 0, lambda q, t: e[tile(q), tile(t)] * rows[tile(q), :], f[...])


def row_pass(y_all, f, e, x, b, fb):
    b[...] = RATIO / jnp.sum(y_all[:, 0], axis=0)
    fb[...] = f[...] * b[...]
    row_totals(x, 0, lambda q, t: e[tile(q), tile(t)] * fb[t : t + 1, :])


def last_col_pass(x_all, f, e, s, y, a, rows):
    a[...] = 1.0 / jnp.sum(x_all[:, 0], axis=0)
    spread_rows(a, rows)
    scale = f[...]
    for t in range(TILES):
        total = jnp.zeros((BLK, BLK), F32)
        scored = jnp.zeros((BLK, BLK), F32)
        for q in range(TILES):
            value = e[tile(q), tile(t)] * rows[tile(q), :]
            total = total + value
            scored = scored + value * s[tile(q), tile(t)]
        put_all(y, 0, t, jnp.sum(total, axis=0, keepdims=True) * scale[t : t + 1, :])
        put_all(y, 1, t, jnp.sum(scored, axis=0, keepdims=True) * scale[t : t + 1, :])


def gu3_pass(y_all, f, a3, e, s, x, b3, gv3, c0, c1):
    b3[...] = RATIO / jnp.sum(y_all[:, 0], axis=0)
    gv3[...] = -b3[...] * jnp.sum(y_all[:, 1], axis=0)
    c1[...] = f[...] * b3[...]
    c0[...] = c1[...] * gv3[...] * (1.0 / RATIO)
    row_totals(
        x, 0, lambda q, t: e[tile(q), tile(t)] * (s[tile(q), tile(t)] * c1[t : t + 1, :] + c0[t : t + 1, :])
    )


def gv_pass(x_all, a, f, b, e, y, rows, agu, *, scale):
    gu = -scale * a[...] * jnp.sum(x_all[:, 0], axis=0)
    agu[...] = a[...] * gu
    spread_rows(agu, rows)
    col_totals(y, 0, lambda q, t: e[tile(q), tile(t)] * rows[tile(q), :], -(f[...] * b[...]))


def gu_pass(y_all, f, b, e, x, bgv, c):
    bgv[...] = b[...] * jnp.sum(y_all[:, 0], axis=0)
    c[...] = f[...] * bgv[...]
    row_totals(x, 0, lambda q, t: e[tile(q), tile(t)] * c[t : t + 1, :])


def captions_kernel(
    pos, x_all, r_a2, r_a3, r_gu2, r_gu3, f, fb0, b2, b3, gv3, bgv2, gv1, e, s, img,
    gs, mine, other, vec, r_gu1, k,
):
    vec[...] = (-INVERSE_EPSILON / RATIO) * jnp.sum(x_all[:, 0], axis=0)
    spread_rows(vec, r_gu1)
    scale = f[...]
    k[0] = -INVERSE_EPSILON * (scale * b3[...])
    k[1] = -(scale * b3[...]) * (1.0 + gv3[...])
    k[2] = -scale * bgv2[...]
    k[3] = -scale * gv1[...]
    k[4] = -INVERSE_EPSILON * (scale * b2[...])
    k[5] = -INVERSE_EPSILON * scale
    k[6] = -fb0[...]

    @pl.loop(0, TILES)
    def _(t):
        columns = pl.ds(pl.multiple_of(t * BLK, BLK), BLK)
        k_s, k_a3, k_a2, k_1, k_gu3, k_gu2, k_gu1 = (k[i, pl.ds(t, 1), :] for i in range(7))
        for q in range(TILES):
            rows = tile(q)
            value = (
                r_a3[rows, :] * (k_a3 + k_s * s[rows, columns])
                + r_a2[rows, :] * k_a2
                + k_1
                + r_gu3[rows, :] * k_gu3
                + r_gu2[rows, :] * k_gu2
                + r_gu1[rows, :] * k_gu1
            )
            gs[rows, columns] = (value * e[rows, columns]).astype(BF16)

    core = pos[4]
    for out, c in ((other, 1 - core), (mine, core)):
        for half in range(2):
            columns = pl.ds(pl.multiple_of(c * 512 + half * 256, 256), 256)
            out[half * 256 : half * 256 + 256, :] = lax.dot_general(
                gs[:, columns], img[...], (((0,), (0,)), ((), ())), preferred_element_type=F32
            ).astype(out.dtype)


def image_rows(pos, gs, cap, k):
    target = lax.rem(pos[3] + k, Y)
    return jnp.dot(gs[pl.ds(target * 256, 256), :], cap[...], preferred_element_type=F32)


def passing_images_kernel(pos, gs, cap, o2a, o2b):
    value = image_rows(pos, gs, cap, 2)
    o2a[...] = value[:BLK].astype(BF16)
    o2b[...] = value[BLK:].astype(BF16)


def images_kernel(pos, gs, cap, o0, o1, o3):
    for k, out in ((1, o1), (3, o3), (0, o0)):
        out[...] = image_rows(pos, gs, cap, k).astype(out.dtype)


def split_over_x(pos, mine, received, p0, p1, p2, p3):
    for k, out in enumerate((p0, p1, p2, p3)):
        rows = pl.ds(lax.rem(pos[0] + k, X) * BLK, BLK)
        out[...] = (mine[rows, :] + received[rows, :].astype(F32)).astype(out.dtype)


def split_over_zh(pos, own, r1, r2, r3, p0, p1, p2, p3):
    for k, out in enumerate((p0, p1, p2, p3)):
        rows = pl.ds(lax.rem(pos[1] + k, ZH) * 32, 32)
        total = own[rows, :]
        for r in (r1, r2, r3):
            total = total + r[rows, :].astype(F32)
        out[...] = total.astype(out.dtype)


def add_passing(o1, o3, passing1, passing3, out1, out3):
    out1[:BLK, :] = (o1[:BLK, :].astype(F32) + passing1[...].astype(F32)).astype(BF16)
    out1[BLK:, :] = o1[BLK:, :]
    out3[:BLK, :] = o3[:BLK, :]
    out3[BLK:, :] = (o3[BLK:, :].astype(F32) + passing3[...].astype(F32)).astype(BF16)


def split_over_zl(pos, own, r1, r3, keep, give):
    zl = pos[2]
    for out, half in ((give, 1 - zl), (keep, zl)):
        rows = pl.ds(half * BLK, BLK)
        out[...] = (own[rows, :] + r1[rows, :].astype(F32) + r3[rows, :].astype(F32)).astype(out.dtype)


def shape(dims, dtype=F32):
    return jax.ShapeDtypeStruct(dims, dtype)


VEC = (TILES, BLK)
ROWS = pltpu.VMEM((SIDE, BLK), F32)
SPREAD = jax.ShapeDtypeStruct((SIDE, BLK), F32)


def run(kernel, outs, scratch, smem, *args, limit=6, aliases={}):
    return pl.pallas_call(
        kernel,
        out_shape=outs,
        in_specs=[SMEM] * smem + [VMEM] * (len(args) - smem),
        out_specs=[VMEM] * len(outs),
        scratch_shapes=scratch,
        input_output_aliases=aliases,
        compiler_params=pltpu.CompilerParams(vmem_limit_bytes=limit * MIB),
    )(*args)


def ring(n, k):
    return [(i, (i + k) % n) for i in range(n)]


def over_txt(v):
    return lax.all_to_all(v, ("y", "zl"), 0, 0, tiled=True)


def over_img(v):
    return lax.all_to_all(v, ("x", "zh", "c"), 0, 0, tiled=True)


def over_img2(v):
    both = v + lax.ppermute(v, "c", ring(C, 1))
    return lax.all_to_all(jnp.broadcast_to(both, (N_IMG // C,) + v.shape[1:]), ("x", "zh"), 0, 0, tiled=True)


def on_device(images, captions, tile_mask):
    pos = jnp.stack([lax.axis_index(name) for name in ("x", "zh", "zl", "y", "c")]).astype(jnp.int32)
    swap = ring(2, 1)
    sibling = lax.ppermute(images, "zl", swap)
    z1, z2, z3 = (lax.ppermute(captions, "zh", ring(ZH, k)) for k in (1, 2, 3))
    m10 = lax.ppermute(tile_mask, "zl", swap)
    m00 = jnp.minimum(tile_mask, 1)
    sibling, z1, z2, z3, m00, m10 = lax.optimization_barrier((sibling, z1, z2, z3, m00, m10))
    m01 = lax.ppermute(tile_mask, "c", swap)
    m11 = lax.ppermute(m10, "c", swap)
    cap_z = jnp.stack([captions, z1, z2, z3])
    c1, c2, c3 = (lax.ppermute(cap_z, "x", ring(X, k)) for k in (1, 2, 3))
    sibling, cap_z = lax.optimization_barrier((sibling, cap_z))
    i0 = jnp.stack([images, sibling])
    i1, i3 = (lax.ppermute(i0, "y", ring(Y, k)) for k in (1, 3))
    c1, c3, i1, i3 = lax.optimization_barrier((c1, c3, i1, i3))
    i2 = lax.ppermute(i1, "y", ring(Y, 1))
    caps = [cap_z, c1, c2, c3]
    other_caps = [lax.ppermute(piece, "c", swap) for piece in caps]

    to_txt = shape((N_TXT, 1) + VEC)
    to_img = shape((N_IMG, 1) + VEC)
    square = (SIDE, SIDE)
    img, cap, s, row_stats, mask = run(
        scores_kernel,
        [shape(square, BF16), shape(square, BF16), shape(square), to_txt, shape((TILES * TILES, BLK))],
        [], 5, pos, m00, m01, m10, m11, i0, i1, i3, *caps, *other_caps, limit=10,
    )
    img, s, row_stats = run(
        last_scores_kernel, [shape(square, BF16), shape(square), to_txt],
        [], 1, pos, i2, cap, mask, img, s, row_stats, limit=10, aliases={4: 0, 5: 1, 6: 2},
    )
    e, col_stats, top = run(
        kernel_matrix, [shape(square), to_img, shape(VEC)],
        [pltpu.VMEM(VEC, F32), ROWS], 0, mask, over_txt(row_stats), s,
    )
    x, f, fb0 = run(first_row_pass, [to_txt, shape(VEC), shape(VEC)], [], 0, over_img(col_stats), top, e)
    y, a2, r_a2 = run(col_pass, [to_img, shape(VEC), SPREAD], [], 0, over_txt(x), f, e)
    vec = pltpu.VMEM(VEC, F32)
    x, b2 = run(row_pass, [to_txt, shape(VEC)], [vec], 0, over_img(y), f, e)
    y, a3, r_a3 = run(last_col_pass, [shape((1, 2) + VEC), shape(VEC), SPREAD], [], 0, over_txt(x), f, e, s)
    x, b3, gv3 = run(gu3_pass, [to_txt, shape(VEC), shape(VEC)], [vec, vec], 0, over_img2(y), f, a3, e, s)
    y, r_gu3 = run(functools.partial(gv_pass, scale=1.0), [to_img, SPREAD], [vec], 0, over_txt(x), a3, f, b2, e)
    x, bgv2 = run(gu_pass, [to_txt, shape(VEC)], [vec], 0, over_img(y), f, b2, e)
    one = jnp.ones(VEC, F32)
    y, r_gu2 = run(functools.partial(gv_pass, scale=1.0 / RATIO), [to_img, SPREAD], [vec], 0, over_txt(x), a2, f, one, e)
    x, gv1 = run(gu_pass, [to_txt, shape(VEC)], [vec], 0, over_img(y), f, one, e)
    gs, mine, other = run(
        captions_kernel, [shape(square, BF16), shape((512, SIDE)), shape((512, SIDE), BF16)],
        [vec, ROWS, pltpu.VMEM((7,) + VEC, F32)], 1,
        pos, over_txt(x), r_a2, r_a3, r_gu2, r_gu3, f, fb0, b2, b3, gv3, bgv2, gv1, e, s, img, limit=10,
    )
    other = lax.ppermute(other, "c", swap)
    block, half, part = (2 * BLK, SIDE), (BLK, SIDE), (32, SIDE)
    o2a, o2b = run(passing_images_kernel, [shape(half, BF16)] * 2, [], 1, pos, gs, cap, limit=10)
    o0, o1, o3 = run(
        images_kernel, [shape(block)] + [shape(block, BF16)] * 2, [], 1, pos, gs, cap, limit=10,
    )
    o2a = lax.ppermute(o2a, "y", ring(Y, 1))
    o2b = lax.ppermute(o2b, "y", ring(Y, 3))
    p0, p1, p2, p3 = run(split_over_x, [shape(half)] + [shape(half, BF16)] * 3, [], 1, pos, mine, other)
    p1, p2, p3 = (lax.ppermute(p, "x", ring(X, k)) for k, p in enumerate((p1, p2, p3), 1))
    o1, o3 = run(add_passing, [shape(block, BF16)] * 2, [], 0, o1, o3, o2a, o2b)
    o1 = lax.ppermute(o1, "y", ring(Y, 1))
    o3 = lax.ppermute(o3, "y", ring(Y, 3))
    keep, give = run(split_over_zl, [shape(half), shape(half, BF16)], [], 1, pos, o0, o1, o3)
    images_grad = keep + lax.ppermute(give, "zl", swap).astype(F32)
    q0, q1, q2, q3 = run(split_over_zh, [shape(part)] + [shape(part, BF16)] * 3, [], 1, pos, p0, p1, p2, p3)
    q1, q2, q3 = (lax.ppermute(q, "zh", ring(ZH, k)) for k, q in enumerate((q1, q2, q3), 1))
    captions_grad = q0 + q1.astype(F32) + q2.astype(F32) + q3.astype(F32)
    return (images_grad, captions_grad)


def solution(mesh):
    split = Mesh(mesh.devices.reshape(X, ZH, ZL, Y, C), ("x", "zh", "zl", "y", "c"))
    img, txt = ("x", "zh", "zl"), ("y", "c")
    in_specs = (P(img + txt, None), P(txt + img, None), P(img, txt))
    out_specs = (P(img + txt, None), P(txt + img, None))
    return jax.shard_map(on_device, mesh=split, in_specs=in_specs, out_specs=out_specs, check_vma=False)
```

```python
import functools

import jax
import jax.numpy as jnp
from jax import lax
from jax.experimental import pallas as pl
from jax.experimental.pallas import tpu as pltpu
from jax.sharding import Mesh, PartitionSpec as P

BLK = 128
INVERSE_EPSILON = 4.0
NEG = -1e30
X, ZH, ZL, Y, C = 4, 4, 2, 4, 2
N_IMG, N_TXT = X * ZH * C, Y * ZL
TILES = 8
SIDE = TILES * BLK
F32, BF16 = jnp.float32, jnp.bfloat16
RATIO = 4.0

VMEM = pl.BlockSpec(memory_space=pltpu.VMEM)
SMEM = pl.BlockSpec(memory_space=pltpu.SMEM)
MIB = 1024 * 1024


def tile(index):
    return pl.ds(index * BLK, BLK)


def spread_rows(vec_ref, out_ref):
    for q in range(TILES):
        row = jnp.broadcast_to(vec_ref[q : q + 1, :], (BLK, BLK))
        out_ref[tile(q), :] = row.T


def put_all(out_ref, slot, q, row):
    for peer in range(out_ref.shape[0]):
        out_ref[peer, slot, q : q + 1, :] = row


def row_totals(out_ref, slot, term):
    for q in range(TILES):
        total = term(q, 0)
        for t in range(1, TILES):
            total = total + term(q, t)
        put_all(out_ref, slot, q, jnp.sum(total.T, axis=0, keepdims=True))


def col_totals(out_ref, slot, term, scale):
    for t in range(TILES):
        total = term(0, t)
        for q in range(1, TILES):
            total = total + term(q, t)
        put_all(out_ref, slot, t, jnp.sum(total, axis=0, keepdims=True) * scale[t : t + 1, :])


def log_sum(top, total):
    return jnp.where(top > NEG, top + jnp.log(total), NEG)


def kept(mask, q, t):
    return jnp.broadcast_to(mask[q * TILES + t : q * TILES + t + 1, :], (BLK, BLK)) > 0


def spread_mask(pos, m00, m01, m10, m11, mask):
    zl, c = pos[2], pos[4]
    left = lax.broadcasted_iota(jnp.int32, (1, BLK), 1) < BLK // 2
    for y in range(Y):
        for dz in range(ZL):
            row = y * 2 + c
            q = y * 2 + jnp.where(dz == 0, zl, 1 - zl)
            for dc, flags in enumerate((m10, m11) if dz else (m00, m01)):
                column = jnp.where(dc == 0, c, 1 - c)
                for x in range(X):
                    lanes = jnp.where(left, flags[row, 2 * x], flags[row, 2 * x + 1])
                    mask[pl.ds(q * TILES + column * X + x, 1), :] = lanes.astype(F32)


def place_images(pos, pieces, k, img):
    source = lax.rem(pos[3] - k + Y, Y)
    for slot in range(2):
        half = jnp.where(slot == 0, pos[2], 1 - pos[2])
        img[pl.ds((source * 2 + half) * BLK, BLK), :] = pieces[slot]
    return source


def score_rows(source, mask, img, cap, s, stats):
    rows = pl.ds(pl.multiple_of(source * 256, 256), 256)
    s[rows, :] = lax.dot_general(
        img[rows, :], cap[...], (((1,), (1,)), ((), ())), preferred_element_type=F32
    )
    for j in range(2):
        q = source * 2 + j
        rows = pl.ds(pl.multiple_of(q * BLK, BLK), BLK)

        def block(t):
            keep = jnp.broadcast_to(mask[pl.ds(q * TILES + t, 1), :], (BLK, BLK)) > 0
            return jnp.where(keep, s[rows, tile(t)] * INVERSE_EPSILON, NEG)

        top = block(0)
        for t in range(1, TILES):
            top = jnp.maximum(top, block(t))
        top_col = jnp.max(top, axis=1, keepdims=True)
        total = jnp.zeros((BLK, BLK), F32)
        for t in range(TILES):
            total = total + jnp.exp(block(t) - top_col)
        value = log_sum(jnp.max(top.T, axis=0, keepdims=True), jnp.sum(total.T, axis=0, keepdims=True))
        for peer in range(N_TXT):
            stats[peer, 0, pl.ds(q, 1), :] = value


def scores_kernel(
    pos, m00, m01, m10, m11, i0, i1, i3, c0, c1, c2, c3, d0, d1, d2, d3, img, cap, s, stats, mask
):
    x, zh, c = pos[0], pos[1], pos[4]
    spread_mask(pos, m00, m01, m10, m11, mask)
    for k, (own, other) in enumerate(((c0, d0), (c1, d1), (c2, d2), (c3, d3))):
        source = lax.rem(x - k + X, X)
        for j in range(ZH):
            place = lax.rem(zh - j + ZH, ZH) * 32
            cap[pl.ds((c * X + source) * BLK + place, 32), :] = own[j]
            cap[pl.ds(((1 - c) * X + source) * BLK + place, 32), :] = other[j]
    for k, pieces in ((0, i0), (1, i1), (3, i3)):
        place_images(pos, pieces, k, img)

    @pl.loop(0, 3)
    def _(j):
        k = j + j // 2
        score_rows(lax.rem(pos[3] - k + Y, Y), mask, img, cap, s, stats)


def last_scores_kernel(pos, i2, cap, mask, img_in, s_in, stats_in, img, s, stats):
    source = place_images(pos, i2, 2, img)
    score_rows(source, mask, img, cap, s, stats)


def joined(stats):
    top = jnp.max(stats[:, 0], axis=0)
    return top, jnp.sum(jnp.exp(stats[:, 0] - top[None]), axis=0)


def kernel_matrix(mask, row_stats, s, e, stats, top_out, u_vec, u_rows):
    top, total = joined(row_stats)
    u_vec[...] = -(top + jnp.log(total))
    spread_rows(u_vec, u_rows)
    @pl.loop(0, TILES, unroll=8)
    def _(t):
        columns = pl.ds(pl.multiple_of(t * BLK, BLK), BLK)

        def masked(q):
            w = s[tile(q), columns] * INVERSE_EPSILON + u_rows[tile(q), :]
            keep = jnp.broadcast_to(mask[pl.ds(q * TILES + t, 1), :], (BLK, BLK)) > 0
            return keep, jnp.where(keep, w, NEG)

        top = masked(0)[1]
        for q in range(1, TILES):
            top = jnp.maximum(top, masked(q)[1])
        top_row = jnp.max(top, axis=0, keepdims=True)
        total = jnp.zeros((BLK, BLK), F32)
        for q in range(TILES):
            keep, w = masked(q)
            value = jnp.where(keep, jnp.exp(w - top_row), 0.0)
            e[tile(q), columns] = value
            total = total + value
        top_out[pl.ds(t, 1), :] = top_row
        value = log_sum(top_row, jnp.sum(total, axis=0, keepdims=True))
        for peer in range(N_IMG):
            stats[peer, 0, pl.ds(t, 1), :] = value


def first_row_pass(col_stats, own_top, e, x, f, fb0):
    top, total = joined(col_stats)
    mine = own_top[...]
    f[...] = RATIO * jnp.exp(mine - top) / total
    fb0[...] = jnp.exp(mine)
    row_totals(x, 0, lambda q, t: e[tile(q), tile(t)] * f[t : t + 1, :])


def col_pass(x_all, f, e, y, a, rows):
    a[...] = 1.0 / jnp.sum(x_all[:, 0], axis=0)
    spread_rows(a, rows)
    col_totals(y, 0, lambda q, t: e[tile(q), tile(t)] * rows[tile(q), :], f[...])


def row_pass(y_all, f, e, x, b, fb):
    b[...] = RATIO / jnp.sum(y_all[:, 0], axis=0)
    fb[...] = f[...] * b[...]
    row_totals(x, 0, lambda q, t: e[tile(q), tile(t)] * fb[t : t + 1, :])


def last_col_pass(x_all, f, e, s, y, a, rows):
    a[...] = 1.0 / jnp.sum(x_all[:, 0], axis=0)
    spread_rows(a, rows)
    scale = f[...]
    for t in range(TILES):
        total = jnp.zeros((BLK, BLK), F32)
        scored = jnp.zeros((BLK, BLK), F32)
        for q in range(TILES):
            value = e[tile(q), tile(t)] * rows[tile(q), :]
            total = total + value
            scored = scored + value * s[tile(q), tile(t)]
        put_all(y, 0, t, jnp.sum(total, axis=0, keepdims=True) * scale[t : t + 1, :])
        put_all(y, 1, t, jnp.sum(scored, axis=0, keepdims=True) * scale[t : t + 1, :])


def gu3_pass(y_all, f, a3, e, s, x, b3, gv3, c0, c1):
    b3[...] = RATIO / jnp.sum(y_all[:, 0], axis=0)
    gv3[...] = -b3[...] * jnp.sum(y_all[:, 1], axis=0)
    c1[...] = f[...] * b3[...]
    c0[...] = c1[...] * gv3[...] * (1.0 / RATIO)
    row_totals(
        x, 0, lambda q, t: e[tile(q), tile(t)] * (s[tile(q), tile(t)] * c1[t : t + 1, :] + c0[t : t + 1, :])
    )


def gv_pass(x_all, a, f, b, e, y, rows, agu, *, scale):
    gu = -scale * a[...] * jnp.sum(x_all[:, 0], axis=0)
    agu[...] = a[...] * gu
    spread_rows(agu, rows)
    col_totals(y, 0, lambda q, t: e[tile(q), tile(t)] * rows[tile(q), :], -(f[...] * b[...]))


def gu_pass(y_all, f, b, e, x, bgv, c):
    bgv[...] = b[...] * jnp.sum(y_all[:, 0], axis=0)
    c[...] = f[...] * bgv[...]
    row_totals(x, 0, lambda q, t: e[tile(q), tile(t)] * c[t : t + 1, :])


def captions_kernel(
    pos, x_all, r_a2, r_a3, r_gu2, r_gu3, f, fb0, b2, b3, gv3, bgv2, gv1, e, s, img,
    gs, mine, other, vec, r_gu1, k,
):
    vec[...] = (-INVERSE_EPSILON / RATIO) * jnp.sum(x_all[:, 0], axis=0)
    spread_rows(vec, r_gu1)
    scale = f[...]
    k[0] = -INVERSE_EPSILON * (scale * b3[...])
    k[1] = -(scale * b3[...]) * (1.0 + gv3[...])
    k[2] = -scale * bgv2[...]
    k[3] = -scale * gv1[...]
    k[4] = -INVERSE_EPSILON * (scale * b2[...])
    k[5] = -INVERSE_EPSILON * scale
    k[6] = -fb0[...]

    @pl.loop(0, TILES)
    def _(t):
        columns = pl.ds(pl.multiple_of(t * BLK, BLK), BLK)
        k_s, k_a3, k_a2, k_1, k_gu3, k_gu2, k_gu1 = (k[i, pl.ds(t, 1), :] for i in range(7))
        for q in range(TILES):
            rows = tile(q)
            value = (
                r_a3[rows, :] * (k_a3 + k_s * s[rows, columns])
                + r_a2[rows, :] * k_a2
                + k_1
                + r_gu3[rows, :] * k_gu3
                + r_gu2[rows, :] * k_gu2
                + r_gu1[rows, :] * k_gu1
            )
            gs[rows, columns] = (value * e[rows, columns]).astype(BF16)

    core = pos[4]
    for out, c in ((other, 1 - core), (mine, core)):
        for half in range(2):
            columns = pl.ds(pl.multiple_of(c * 512 + half * 256, 256), 256)
            out[half * 256 : half * 256 + 256, :] = lax.dot_general(
                gs[:, columns], img[...], (((0,), (0,)), ((), ())), preferred_element_type=F32
            ).astype(out.dtype)


def image_rows(pos, gs, cap, k):
    target = lax.rem(pos[3] + k, Y)
    return jnp.dot(gs[pl.ds(target * 256, 256), :], cap[...], preferred_element_type=F32)


def passing_images_kernel(pos, gs, cap, o2a, o2b):
    value = image_rows(pos, gs, cap, 2)
    o2a[...] = value[:BLK].astype(BF16)
    o2b[...] = value[BLK:].astype(BF16)


def images_kernel(pos, gs, cap, o0, o1, o3):
    for k, out in ((1, o1), (3, o3), (0, o0)):
        out[...] = image_rows(pos, gs, cap, k).astype(out.dtype)


def split_over_x(pos, mine, received, p0, p1, p2, p3):
    for k, out in enumerate((p0, p1, p2, p3)):
        rows = pl.ds(lax.rem(pos[0] + k, X) * BLK, BLK)
        out[...] = (mine[rows, :] + received[rows, :].astype(F32)).astype(out.dtype)


def split_over_zh(pos, own, r1, r2, r3, p0, p1, p2, p3):
    for k, out in enumerate((p0, p1, p2, p3)):
        rows = pl.ds(lax.rem(pos[1] + k, ZH) * 32, 32)
        total = own[rows, :]
        for r in (r1, r2, r3):
            total = total + r[rows, :].astype(F32)
        out[...] = total.astype(out.dtype)


def add_passing(o1, o3, passing1, passing3, out1, out3):
    out1[:BLK, :] = (o1[:BLK, :].astype(F32) + passing1[...].astype(F32)).astype(BF16)
    out1[BLK:, :] = o1[BLK:, :]
    out3[:BLK, :] = o3[:BLK, :]
    out3[BLK:, :] = (o3[BLK:, :].astype(F32) + passing3[...].astype(F32)).astype(BF16)


def split_over_zl(pos, own, r1, r3, keep, give):
    zl = pos[2]
    for out, half in ((give, 1 - zl), (keep, zl)):
        rows = pl.ds(half * BLK, BLK)
        out[...] = (own[rows, :] + r1[rows, :].astype(F32) + r3[rows, :].astype(F32)).astype(out.dtype)


def shape(dims, dtype=F32):
    return jax.ShapeDtypeStruct(dims, dtype)


VEC = (TILES, BLK)
ROWS = pltpu.VMEM((SIDE, BLK), F32)
SPREAD = jax.ShapeDtypeStruct((SIDE, BLK), F32)


def run(kernel, outs, scratch, smem, *args, limit=6, aliases={}):
    return pl.pallas_call(
        kernel,
        out_shape=outs,
        in_specs=[SMEM] * smem + [VMEM] * (len(args) - smem),
        out_specs=[VMEM] * len(outs),
        scratch_shapes=scratch,
        input_output_aliases=aliases,
        compiler_params=pltpu.CompilerParams(vmem_limit_bytes=limit * MIB),
    )(*args)


def ring(n, k):
    return [(i, (i + k) % n) for i in range(n)]


def over_txt(v):
    return lax.all_to_all(v, ("y", "zl"), 0, 0, tiled=True)


def over_img(v):
    return lax.all_to_all(v, ("x", "zh", "c"), 0, 0, tiled=True)


def over_img2(v):
    both = v + lax.ppermute(v, "c", ring(C, 1))
    return lax.all_to_all(jnp.broadcast_to(both, (N_IMG // C,) + v.shape[1:]), ("x", "zh"), 0, 0, tiled=True)


def on_device(images, captions, tile_mask):
    pos = jnp.stack([lax.axis_index(name) for name in ("x", "zh", "zl", "y", "c")]).astype(jnp.int32)
    swap = ring(2, 1)
    sibling = lax.ppermute(images, "zl", swap)
    z1, z2, z3 = (lax.ppermute(captions, "zh", ring(ZH, k)) for k in (1, 2, 3))
    m10 = lax.ppermute(tile_mask, "zl", swap)
    m00 = jnp.minimum(tile_mask, 1)
    sibling, z1, z2, z3, m00, m10 = lax.optimization_barrier((sibling, z1, z2, z3, m00, m10))
    m01 = lax.ppermute(tile_mask, "c", swap)
    m11 = lax.ppermute(m10, "c", swap)
    cap_z = jnp.stack([captions, z1, z2, z3])
    c1, c2, c3 = (lax.ppermute(cap_z, "x", ring(X, k)) for k in (1, 2, 3))
    sibling, cap_z = lax.optimization_barrier((sibling, cap_z))
    i0 = jnp.stack([images, sibling])
    i1, i3 = (lax.ppermute(i0, "y", ring(Y, k)) for k in (1, 3))
    c1, c3, i1, i3 = lax.optimization_barrier((c1, c3, i1, i3))
    i2 = lax.ppermute(i1, "y", ring(Y, 1))
    caps = [cap_z, c1, c2, c3]
    other_caps = [lax.ppermute(piece, "c", swap) for piece in caps]

    to_txt = shape((N_TXT, 1) + VEC)
    to_img = shape((N_IMG, 1) + VEC)
    square = (SIDE, SIDE)
    img, cap, s, row_stats, mask = run(
        scores_kernel,
        [shape(square, BF16), shape(square, BF16), shape(square), to_txt, shape((TILES * TILES, BLK))],
        [], 5, pos, m00, m01, m10, m11, i0, i1, i3, *caps, *other_caps, limit=10,
    )
    img, s, row_stats = run(
        last_scores_kernel, [shape(square, BF16), shape(square), to_txt],
        [], 1, pos, i2, cap, mask, img, s, row_stats, limit=10, aliases={4: 0, 5: 1, 6: 2},
    )
    e, col_stats, top = run(
        kernel_matrix, [shape(square), to_img, shape(VEC)],
        [pltpu.VMEM(VEC, F32), ROWS], 0, mask, over_txt(row_stats), s,
    )
    x, f, fb0 = run(first_row_pass, [to_txt, shape(VEC), shape(VEC)], [], 0, over_img(col_stats), top, e)
    y, a2, r_a2 = run(col_pass, [to_img, shape(VEC), SPREAD], [], 0, over_txt(x), f, e)
    vec = pltpu.VMEM(VEC, F32)
    x, b2 = run(row_pass, [to_txt, shape(VEC)], [vec], 0, over_img(y), f, e)
    y, a3, r_a3 = run(last_col_pass, [shape((1, 2) + VEC), shape(VEC), SPREAD], [], 0, over_txt(x), f, e, s)
    x, b3, gv3 = run(gu3_pass, [to_txt, shape(VEC), shape(VEC)], [vec, vec], 0, over_img2(y), f, a3, e, s)
    y, r_gu3 = run(functools.partial(gv_pass, scale=1.0), [to_img, SPREAD], [vec], 0, over_txt(x), a3, f, b2, e)
    x, bgv2 = run(gu_pass, [to_txt, shape(VEC)], [vec], 0, over_img(y), f, b2, e)
    one = jnp.ones(VEC, F32)
    y, r_gu2 = run(functools.partial(gv_pass, scale=1.0 / RATIO), [to_img, SPREAD], [vec], 0, over_txt(x), a2, f, one, e)
    x, gv1 = run(gu_pass, [to_txt, shape(VEC)], [vec], 0, over_img(y), f, one, e)
    gs, mine, other = run(
        captions_kernel, [shape(square, BF16), shape((512, SIDE)), shape((512, SIDE), BF16)],
        [vec, ROWS, pltpu.VMEM((7,) + VEC, F32)], 1,
        pos, over_txt(x), r_a2, r_a3, r_gu2, r_gu3, f, fb0, b2, b3, gv3, bgv2, gv1, e, s, img, limit=10,
    )
    other = lax.ppermute(other, "c", swap)
    block, half, part = (2 * BLK, SIDE), (BLK, SIDE), (32, SIDE)
    o2a, o2b = run(passing_images_kernel, [shape(half, BF16)] * 2, [], 1, pos, gs, cap, limit=10)
    o0, o1, o3 = run(
        images_kernel, [shape(block)] + [shape(block, BF16)] * 2, [], 1, pos, gs, cap, limit=10,
    )
    o2a = lax.ppermute(o2a, "y", ring(Y, 1))
    o2b = lax.ppermute(o2b, "y", ring(Y, 3))
    p0, p1, p2, p3 = run(split_over_x, [shape(half)] + [shape(half, BF16)] * 3, [], 1, pos, mine, other)
    p1, p2, p3 = (lax.ppermute(p, "x", ring(X, k)) for k, p in enumerate((p1, p2, p3), 1))
    o2a, o2b, p1, p3 = lax.optimization_barrier((o2a, o2b, p1, p3))
    o1, o3 = run(add_passing, [shape(block, BF16)] * 2, [], 0, o1, o3, o2a, o2b)
    o1 = lax.ppermute(o1, "y", ring(Y, 1))
    o3 = lax.ppermute(o3, "y", ring(Y, 3))
    keep, give = run(split_over_zl, [shape(half), shape(half, BF16)], [], 1, pos, o0, o1, o3)
    q0, q1, q2, q3 = run(split_over_zh, [shape(part)] + [shape(part, BF16)] * 3, [], 1, pos, p0, p1, p2, p3)
    q2, q3, give = lax.optimization_barrier((q2, q3, give))
    q1, q2, q3 = (lax.ppermute(q, "zh", ring(ZH, k)) for k, q in enumerate((q1, q2, q3), 1))
    images_grad = keep + lax.ppermute(give, "zl", swap).astype(F32)
    images_grad, q1, q2, q3 = lax.optimization_barrier((images_grad, q1, q2, q3))
    captions_grad = q0 + q1.astype(F32) + q2.astype(F32) + q3.astype(F32)
    return (images_grad, captions_grad)


def solution(mesh):
    split = Mesh(mesh.devices.reshape(X, ZH, ZL, Y, C), ("x", "zh", "zl", "y", "c"))
    img, txt = ("x", "zh", "zl"), ("y", "c")
    in_specs = (P(img + txt, None), P(txt + img, None), P(img, txt))
    out_specs = (P(img + txt, None), P(txt + img, None))
    return jax.shard_map(on_device, mesh=split, in_specs=in_specs, out_specs=out_specs, check_vma=False)
```
